32 devices in a mesh: dp: 8 (over y, x, core), mp: 4 (over z).
Axes of the slice: x: 2, y: 2, z: 4, core: 2. Of those that a mesh axis runs over, the one named last changes fastest.
Arguments:
- pool: bfloat16 [64, 32, 5120], P('dp', None, 'mp'), may hold values from -20 to 20
- send_table: int32 [8, 8], P('dp'), may hold values from -1 to 7, as said below
- slot_source: int32 [64], P('dp'), may hold values from 0 to 7, as said below
- multiplicity: int32 [64], P('dp'), may hold values from 1 to 4
- slot_weight: float32 [64], P('dp'), may hold values from 0.1 to 1
- cotangent: bfloat16 [64, 32, 4096], P('dp', None, 'mp'), may hold values from -6 to 6
- w_query: bfloat16 [5120, 4096], P(None, 'mp'), may hold values from -0.078125 to 0.078125
- w_key: bfloat16 [5120, 512], P('mp'), may hold values from -0.078125 to 0.078125
- w_value: bfloat16 [5120, 512], P('mp'), may hold values from -0.078125 to 0.078125
- query_gain: float32 [128], replicated, may hold values from 0.5 to 5
- key_gain: float32 [128], replicated, may hold values from 0.5 to 5
Outputs:
- attended: bfloat16 [64, 32, 4096], P('dp', None, 'mp')
- grad_query: float32 [5120, 4096], P('dp', 'mp')
- key_gradient: float32 [5120, 512], P('mp', 'dp')
- grad_value: float32 [5120, 512], P('mp', 'dp')
The draws below stay inside these ranges and needn't reach their ends.
Inputs may be any that keep to these rules, and one draw needn't show every extreme that they name: Entry [r, d] is the sequence of rank r's pool of 8 that data rank d receives from rank r, or -1 where rank d takes nothing from rank r; send_table[r, d] >= 0 exactly where r is among the sources of rank d's slots. `slot_source`: the 8 slots of data rank d (entries d * 8 to d * 8 + 7) name 8 different source ranks.
All inputs are finite; a program needn't handle non-finite values.
Results may differ from the reference program's by a relative error of at most 0.025.
The reference program's roundings to bfloat16 on the way count: a program that leaves them out, or rounds other values in their place, can miss the bound.
Values may be sent and summed in bfloat16 or wider, within the bound.
No kernel may reach another device: no remote copies, remote signals or barrier semaphores. Data moves between devices by JAX's collectives and lax.ppermute only.
A program may use at most 64 MiB of HBM per device.

```python
import math
import jax
import jax.numpy as jnp
from jax import lax

D = 5120
HEAD_DIM = 128
HEADS = 32
KV_HEADS = 4
LENGTH = 32
SLOTS = 8
POOL = 8
SEQS = 64
SAMPLES = 64
N_DP = 8


def sample_plan(key):
    score_key, forced_key, pick_key, spot_key, popular_key = jax.random.split(key, 5)
    usage_frequency = jax.random.randint(popular_key, (N_DP,), 1, 9)
    random_jitter = jax.random.randint(score_key, (N_DP, N_DP), 0, 65536)
    pinned_choice = jax.random.permutation(forced_key, N_DP)
    source_index = jnp.arange(N_DP, dtype=jnp.int32)
    extra_reward = jnp.where(source_index[None, :] == pinned_choice[:, None], 1 << 20, 0)
    score_matrix = (random_jitter * usage_frequency[None, :] + extra_reward) * N_DP + source_index[None, :]
    ignored, sources = lax.top_k(score_matrix, SLOTS)
    picks = jax.random.randint(pick_key, (N_DP, SLOTS), 0, POOL)
    row_key, col_key = jax.random.split(spot_key)
    spot_row = jax.random.randint(row_key, (), 0, N_DP)
    spot_col = jax.random.randint(col_key, (), 0, SLOTS)
    picks = picks.at[spot_row, spot_col].set(POOL - 1)
    return (sources.astype(jnp.int32), picks.astype(jnp.int32))


def draw_send_table(key, part):
    sources, picks = sample_plan(key)
    columns = jnp.broadcast_to(jnp.arange(N_DP, dtype=jnp.int32)[:, None], (N_DP, SLOTS))
    table = jnp.full((N_DP, N_DP), -1, jnp.int32)
    return table.at[sources, columns].set(picks)


def draw_slot_source(key, part):
    sources, picks = sample_plan(key)
    return sources.reshape(-1).astype(jnp.int32)


def draw_pool(key, part):
    key = jax.random.fold_in(key, 5)
    first, second = jax.random.split(key)
    scale = jnp.exp(jax.random.uniform(first, (SEQS, LENGTH, 1), jnp.float32, -1.15, 1.15))
    values = jnp.clip(jax.random.normal(second, (SEQS, LENGTH, D), jnp.float32), -6.0, 6.0)
    return (scale * values).astype(jnp.bfloat16)


def gain_values(key, lower, upper):
    return jax.random.uniform(key, (HEAD_DIM,), jnp.float32, lower, upper)


def draw_query_gain(key, part):
    key = jax.random.fold_in(key, 3)
    return gain_values(key, 0.5, 1.5)


def draw_key_gain(key, part):
    key = jax.random.fold_in(key, 4)
    return gain_values(key, 0.5, 1.5)


def touch_ends(values, rng, smallest, top_value):
    dims = values.shape
    place = [jax.random.randint(jax.random.fold_in(rng, axis), (), 0, dims[axis]) for axis in range(len(dims))]
    values = values.at[tuple(place)].set(smallest)
    longest = dims.index(max(dims))
    place[longest] = (place[longest] + 1) % dims[longest]
    return values.at[tuple(place)].set(top_value)


def levels(rng, extent, cuts, low, high):
    loudness, own = 1.0, jax.random.fold_in(rng, 6)
    for dim, shards_of in cuts:
        draws = jnp.exp(jax.random.uniform(jax.random.fold_in(own, dim), (shards_of,), jnp.float32, low / len(cuts), high / len(cuts)))
        loudness = loudness * jnp.repeat(draws, extent[dim] // shards_of).reshape([-1 if axis == dim else 1 for axis in range(len(extent))])
    return loudness


def noise(own_key, dims, scale, bound, cuts=(), held_as=jnp.bfloat16):
    factor_of = levels(own_key, dims, cuts, -0.22, 0.18) if cuts else 1.0
    result = jax.random.normal(own_key, dims, jnp.float32) * scale * factor_of
    return jnp.minimum(jnp.maximum(result, -bound), bound).astype(held_as)


def setup_inputs(seed: int = 0) -> dict:
    arg_keys = jax.random.split(jax.random.key(seed), 12)
    pool = draw_pool(jax.random.fold_in(arg_keys[11], 71), 0)
    send_table = draw_send_table(jax.random.fold_in(arg_keys[11], 71), 0)
    slot_source = draw_slot_source(jax.random.fold_in(arg_keys[11], 71), 0)
    multiplicity = touch_ends(jax.random.randint(arg_keys[3], (SAMPLES,), 1, 5), jax.random.fold_in(arg_keys[3], 1), 1, 4).astype(jnp.int32)
    slot_weight = jnp.clip(jnp.exp(math.log(1.0) - 2.3025851 * jax.random.uniform(arg_keys[4], (SAMPLES,), jnp.float32) ** levels(arg_keys[4], (SAMPLES,), ((0, 8),), -0.2, 0.2)), 0.1, 1.0)
    cotangent = noise(arg_keys[5], (SAMPLES, LENGTH, HEADS * HEAD_DIM), 1.0, 6.0, ((0, 8), (2, 4)))
    w_query = noise(arg_keys[6], (D, HEADS * HEAD_DIM), D ** -0.5, 0.078125, ((1, 4),))
    w_key = noise(arg_keys[7], (D, KV_HEADS * HEAD_DIM), D ** -0.5, 0.078125, ((0, 4),))
    w_value = noise(arg_keys[8], (D, KV_HEADS * HEAD_DIM), D ** -0.5, 0.078125, ((0, 4),))
    query_gain = draw_query_gain(jax.random.fold_in(arg_keys[11], 71), 0)
    key_gain = draw_key_gain(jax.random.fold_in(arg_keys[11], 71), 0)
    return dict(pool=pool, send_table=send_table, slot_source=slot_source, multiplicity=multiplicity, slot_weight=slot_weight, cotangent=cotangent, w_query=w_query, w_key=w_key, w_value=w_value, query_gain=query_gain, key_gain=key_gain)


def rms_scale(values, gain):
    inverse = lax.rsqrt(lax.optimization_barrier(jnp.mean(values * values, axis=-1, keepdims=True)) + 1e-06)
    return (values * inverse * gain, inverse)

def rms_back(values, inverse, gain, grad_out):
    scaled = grad_out * gain
    inner = lax.optimization_barrier(jnp.mean(values * scaled, axis=-1, keepdims=True))
    return inverse * scaled - values * (inverse * inverse * inverse) * inner

def forward_core(query, key_sum, value_sum, query_gain, key_gain):
    scale = 1.0 / math.sqrt(query.shape[-1])
    q_norm, q_inverse = rms_scale(query, query_gain)
    k_norm, k_inverse = rms_scale(key_sum, key_gain)
    q_half = q_norm.astype(jnp.bfloat16)
    k_half = k_norm.astype(jnp.bfloat16)
    v_half = value_sum.astype(jnp.bfloat16)
    score_matrix = jnp.einsum('sqgph,skgh->sgpqk', q_half.astype(jnp.float32), k_half.astype(jnp.float32)) * scale
    length = query.shape[1]
    causal = lax.broadcasted_iota(jnp.int32, (length, length), 0) >= lax.broadcasted_iota(jnp.int32, (length, length), 1)
    score_matrix = jnp.where(causal, score_matrix, -1e+30)
    peak = lax.optimization_barrier(jnp.max(score_matrix, axis=-1, keepdims=True))
    raised = jnp.exp(score_matrix - peak)
    probs = raised / lax.optimization_barrier(jnp.sum(raised, axis=-1, keepdims=True))
    p_half = probs.astype(jnp.bfloat16)
    attended = jnp.einsum('sgpqk,skgh->sqgph', p_half.astype(jnp.float32), v_half.astype(jnp.float32))
    return (attended, (q_inverse, k_inverse, q_half, k_half, v_half, probs, p_half))

def backward_core(d_out, query, key_sum, query_gain, key_gain, saved):
    q_inverse, k_inverse, q_half, k_half, v_half, probs, p_half = saved
    scale = 1.0 / math.sqrt(query.shape[-1])
    out_half = d_out.astype(jnp.bfloat16).astype(jnp.float32)
    d_probs = jnp.einsum('sqgph,skgh->sgpqk', out_half, v_half.astype(jnp.float32))
    d_value = jnp.einsum('sgpqk,sqgph->skgh', p_half.astype(jnp.float32), out_half)
    d_scores = probs * (d_probs - lax.optimization_barrier(jnp.sum(d_probs * probs, axis=-1, keepdims=True))) * scale
    score_half = d_scores.astype(jnp.bfloat16).astype(jnp.float32)
    d_qnorm = jnp.einsum('sgpqk,skgh->sqgph', score_half, k_half.astype(jnp.float32))
    d_knorm = jnp.einsum('sgpqk,sqgph->skgh', score_half, q_half.astype(jnp.float32))
    d_query = rms_back(query, q_inverse, query_gain, d_qnorm)
    d_key = rms_back(key_sum, k_inverse, key_gain, d_knorm)
    return (d_query, d_key, d_value)

def rounded(term):
    half = lax.optimization_barrier(term.astype(jnp.bfloat16))
    return half.astype(jnp.float32)

def reference(pool, send_table, slot_source, multiplicity, slot_weight, cotangent, w_query, w_key, w_value, query_gain, key_gain):
    group_size = HEADS // KV_HEADS
    query_cols = HEADS * HEAD_DIM
    key_cols = KV_HEADS * HEAD_DIM
    token_count = SLOTS * LENGTH
    destination = (jnp.arange(SAMPLES, dtype=jnp.int32) // SLOTS).astype(jnp.int32)
    local_index = send_table[slot_source, destination]
    pool_row = (slot_source * POOL + local_index).astype(jnp.int32)
    factor = multiplicity.astype(jnp.float32) * slot_weight / LENGTH

    def rank_step(carry, inputs):
        grad_query, key_gradient, grad_value = carry
        row_index, cot_rank, factor_rank = inputs
        chosen = jnp.take(pool, row_index, axis=0)
        flat = chosen.reshape(token_count, D)
        query = jnp.dot(flat, w_query, preferred_element_type=jnp.float32).reshape(SLOTS, LENGTH, KV_HEADS, group_size, HEAD_DIM)
        key_sum = jnp.dot(flat, w_key, preferred_element_type=jnp.float32).reshape(SLOTS, LENGTH, KV_HEADS, HEAD_DIM)
        value_sum = jnp.dot(flat, w_value, preferred_element_type=jnp.float32).reshape(SLOTS, LENGTH, KV_HEADS, HEAD_DIM)
        attended, saved = forward_core(query, key_sum, value_sum, query_gain, key_gain)
        d_out = cot_rank.astype(jnp.float32).reshape(SLOTS, LENGTH, KV_HEADS, group_size, HEAD_DIM) * factor_rank[:, None, None, None, None]
        d_query, d_key, d_value = backward_core(d_out, query, key_sum, query_gain, key_gain, saved)
        query_rows = d_query.reshape(token_count, query_cols).astype(jnp.bfloat16)
        key_rows = d_key.reshape(token_count, key_cols).astype(jnp.bfloat16)
        value_rows = d_value.reshape(token_count, key_cols).astype(jnp.bfloat16)
        grad_query = grad_query + rounded(jnp.dot(flat.T, query_rows, preferred_element_type=jnp.float32))
        key_gradient = key_gradient + rounded(jnp.dot(flat.T, key_rows, preferred_element_type=jnp.float32))
        grad_value = grad_value + rounded(jnp.dot(flat.T, value_rows, preferred_element_type=jnp.float32))
        return ((grad_query, key_gradient, grad_value), attended.reshape(SLOTS, LENGTH, query_cols).astype(jnp.bfloat16))
    start = (jnp.zeros((D, query_cols), jnp.float32), jnp.zeros((D, key_cols), jnp.float32), jnp.zeros((D, key_cols), jnp.float32))
    scanned = (pool_row.reshape(N_DP, SLOTS), cotangent.reshape(N_DP, SLOTS, LENGTH, query_cols), factor.reshape(N_DP, SLOTS))
    (grad_query, key_gradient, grad_value), attended = lax.scan(rank_step, start, scanned)
    return (attended.reshape(SAMPLES, LENGTH, query_cols), grad_query, key_gradient, grad_value)
```

```python
import functools
import math

import jax
import jax.numpy as jnp
from jax import lax
from jax.sharding import PartitionSpec as P

HEADS = 32
KV_HEADS = 4
F32 = jnp.float32
BF16 = jnp.bfloat16


def rms_scale(values, gain):
    inverse = lax.rsqrt(jnp.mean(values * values, axis=-1, keepdims=True) + 1e-06)
    return (values * inverse * gain, inverse)


def rms_back(values, inverse, gain, grad_out):
    scaled = grad_out * gain
    inner = jnp.mean(values * scaled, axis=-1, keepdims=True)
    return inverse * scaled - values * (inverse * inverse * inverse) * inner


def forward_core(query, key_sum, value_sum, query_gain, key_gain):
    scale = 1.0 / math.sqrt(query.shape[-1])
    q_norm, q_inverse = rms_scale(query, query_gain)
    k_norm, k_inverse = rms_scale(key_sum, key_gain)
    q_half = q_norm.astype(jnp.bfloat16)
    k_half = k_norm.astype(jnp.bfloat16)
    v_half = value_sum.astype(jnp.bfloat16)
    score_matrix = (
        jnp.einsum("sqgph,skgh->sgpqk", q_half, k_half, preferred_element_type=jnp.float32) * scale
    )
    length = query.shape[1]
    causal = lax.broadcasted_iota(jnp.int32, (length, length), 0) >= lax.broadcasted_iota(
        jnp.int32, (length, length), 1
    )
    score_matrix = jnp.where(causal, score_matrix, -1e30)
    peak = jnp.max(score_matrix, axis=-1, keepdims=True)
    raised = jnp.exp(score_matrix - peak)
    probs = raised / jnp.sum(raised, axis=-1, keepdims=True)
    p_half = probs.astype(jnp.bfloat16)
    attended = jnp.einsum("sgpqk,skgh->sqgph", p_half, v_half, preferred_element_type=jnp.float32)
    return (attended, (q_inverse, k_inverse, q_half, k_half, v_half, probs, p_half))


def backward_core(d_out, query, key_sum, query_gain, key_gain, saved):
    q_inverse, k_inverse, q_half, k_half, v_half, probs, p_half = saved
    scale = 1.0 / math.sqrt(query.shape[-1])
    out_half = d_out.astype(jnp.bfloat16)
    d_probs = jnp.einsum("sqgph,skgh->sgpqk", out_half, v_half, preferred_element_type=jnp.float32)
    d_value = jnp.einsum("sgpqk,sqgph->skgh", p_half, out_half, preferred_element_type=jnp.float32)
    d_scores = probs * (d_probs - jnp.sum(d_probs * probs, axis=-1, keepdims=True)) * scale
    score_half = d_scores.astype(jnp.bfloat16)
    d_qnorm = jnp.einsum(
        "sgpqk,skgh->sqgph", score_half, k_half, preferred_element_type=jnp.float32
    )
    d_knorm = jnp.einsum(
        "sgpqk,sqgph->skgh", score_half, q_half, preferred_element_type=jnp.float32
    )
    d_query = rms_back(query, q_inverse, query_gain, d_qnorm)
    d_key = rms_back(key_sum, k_inverse, key_gain, d_knorm)
    return (d_query, d_key, d_value)


def attend(x, w_query, w_kv, cot, factor, query_gain, key_gain, length, device_cols):
    blocks, tokens, width = x.shape
    dim = query_gain.shape[0]
    slots = tokens // length
    heads = w_query.shape[1] // dim
    x = x.transpose(1, 0, 2).reshape(tokens, blocks * width)
    query = jnp.dot(x, w_query, preferred_element_type=F32)
    kv = jnp.dot(x, w_kv, preferred_element_type=F32)
    query = query.reshape(slots, length, 1, heads, dim)
    key = kv[:, :dim].reshape(slots, length, 1, dim)
    value = kv[:, dim:].reshape(slots, length, 1, dim)
    attended, saved = forward_core(query, key, value, query_gain, key_gain)
    d_out = cot.astype(F32).reshape(slots, length, 1, heads, dim)
    d_out = d_out * factor[:, None, None, None, None]
    d_query, d_key, d_value = backward_core(d_out, query, key, query_gain, key_gain, saved)
    pairs = [d_key.reshape(tokens, -1, device_cols), d_value.reshape(tokens, -1, device_cols)]
    d_kv = jnp.stack(pairs, axis=2).reshape(tokens, 2 * dim)
    return (
        attended.reshape(tokens, -1).astype(BF16),
        d_query.reshape(tokens, -1).astype(BF16),
        d_kv.astype(BF16),
    )


def line_gather(block, axis, count):
    me = lax.axis_index(axis)
    up, down = [block], [block]
    for hop in range(1, count):
        up.append(lax.ppermute(up[-1], axis, [(i, i + 1) for i in range(hop - 1, count - 1)]))
        down.append(
            lax.ppermute(down[-1], axis, [(i, i - 1) for i in range(count - hop, 0, -1)])
        )
    return [block] + [jnp.where(me >= hop, up[hop], down[count - hop]) for hop in range(1, count)]


def pick(array, index):
    return array.at[index].get(mode="promise_in_bounds")


def flip(block, axis, count, bits):
    return lax.ppermute(block, axis, [(i, i ^ bits) for i in range(count)])


def local(
    n_dp,
    n_mp,
    pool,
    send_table,
    slot_source,
    multiplicity,
    slot_weight,
    cotangent,
    w_query,
    w_key,
    w_value,
    query_gain,
    key_gain,
):
    slots = slot_source.shape[0]
    length = pool.shape[1]
    width = pool.shape[2]
    query_cols = w_query.shape[1]
    key_cols = w_key.shape[1]
    dim = query_gain.shape[0]
    tokens = slots * length
    chips = n_dp // 2
    dp = lax.axis_index("dp")
    mp = lax.axis_index("mp")
    chip, core = dp // 2, dp % 2

    share = width // n_dp
    own_key = lax.dynamic_slice_in_dim(w_key, dp * share, share, 0)
    own_value = lax.dynamic_slice_in_dim(w_value, dp * share, share, 0)
    pairs = []
    for i in range(n_mp):
        head = i * KV_HEADS // n_mp
        columns = slice(head * dim, (head + 1) * dim)
        pairs.append(jnp.concatenate([own_key[:, columns], own_value[:, columns]], axis=1))
    both = jnp.stack(pairs)
    both = lax.all_to_all(both, "mp", split_axis=0, concat_axis=0, tiled=True)
    shares = jnp.stack([both] + [flip(both, "dp", n_dp, 2 * k) for k in range(1, chips)])
    shares = jnp.stack([shares, flip(shares, "dp", n_dp, 1)], axis=1)
    shares = shares.reshape(n_dp, n_mp, share, 2 * dim)
    shares = pick(shares, dp ^ jnp.arange(n_dp))
    w_kv = shares.transpose(1, 0, 2, 3).reshape(n_mp * width, 2 * dim)

    outgoing = pick(pool, jnp.maximum(send_table[0], 0))
    arrived = lax.all_to_all(outgoing, "dp", split_axis=0, concat_axis=0, tiled=True)
    rows = pick(arrived, slot_source).reshape(tokens, width)

    if n_mp <= 4:
        near = jnp.stack(line_gather(rows, "mp", n_mp))
        x = pick(near, (mp - jnp.arange(n_mp)) % n_mp)
    else:
        x = lax.all_gather(rows, "mp", axis=0)

    plane_rows = jnp.stack([rows] + [flip(rows, "dp", n_dp, 2 * k) for k in range(1, chips)])
    plane_rows = plane_rows.reshape(chips * tokens, width)

    chip_width = n_mp * width // chips
    if chip_width == width:
        parts = x
    else:
        parts = x.transpose(1, 0, 2).reshape(tokens, chips, chip_width).transpose(1, 0, 2)
    part = lambda k: lax.dynamic_index_in_dim(parts, chip ^ k, 0, keepdims=False)
    chip_rows = jnp.stack([part(0)] + [flip(part(k), "dp", n_dp, 2 * k) for k in range(1, chips)])
    chip_rows = chip_rows.reshape(chips * tokens, chip_width)

    factor = multiplicity.astype(F32) * slot_weight / length
    attended, d_query, d_kv = attend(
        x,
        w_query,
        w_kv,
        cotangent.reshape(tokens, query_cols),
        factor,
        query_gain,
        key_gain,
        length,
        key_cols // n_dp,
    )

    d_all = jnp.stack([d_query] + [flip(d_query, "dp", n_dp, 2 * k) for k in range(1, chips)])
    d_all = d_all.reshape(chips * tokens, query_cols)
    half = chip_width // 2

    def query_half(which):
        mine = lax.dynamic_slice_in_dim(chip_rows, which * half, half, 1)
        return jnp.einsum("td,tc->dc", mine, d_all, preferred_element_type=F32)

    other = flip(query_half(1 - core).astype(BF16), "dp", n_dp, 1)
    grad_query = query_half(core) + other.astype(F32)

    spread = jnp.broadcast_to(d_kv[None], (n_mp,) + d_kv.shape)
    spread = lax.all_to_all(spread, "mp", split_axis=0, concat_axis=0, tiled=True)
    if n_mp > KV_HEADS:
        spread = spread.reshape(KV_HEADS, n_mp // KV_HEADS, tokens, 2 * dim)
        spread = jnp.sum(spread.astype(F32), axis=1).astype(BF16)
    chip_cols = 2 * key_cols // chips
    if chip_cols != 2 * dim:
        spread = spread.reshape(KV_HEADS, tokens, chips // KV_HEADS, chip_cols)
        spread = spread.transpose(0, 2, 1, 3).reshape(chips, tokens, chip_cols)
    kv_part = lambda k: lax.dynamic_index_in_dim(spread, chip ^ k, 0, keepdims=False)
    kv_all = jnp.stack([kv_part(0)] + [flip(kv_part(k), "dp", n_dp, 2 * k) for k in range(1, chips)])
    kv_all = kv_all.reshape(chips * tokens, chip_cols)
    partial = jnp.einsum("td,tc->dc", plane_rows, kv_all, preferred_element_type=F32)
    mine, theirs = partial[:, : chip_cols // 2], partial[:, chip_cols // 2 :]
    mine, theirs = jnp.where(core == 0, mine, theirs), jnp.where(core == 0, theirs, mine)
    grad_kv = mine + flip(theirs.astype(BF16), "dp", n_dp, 1).astype(F32)
    device_cols = chip_cols // 4

    return (
        attended.reshape(slots, length, query_cols),
        grad_query,
        grad_kv[:, :device_cols],
        grad_kv[:, device_cols:],
    )


def solution(mesh):
    return jax.shard_map(
        functools.partial(local, mesh.shape["dp"], mesh.shape["mp"]),
        mesh=mesh,
        in_specs=(
            P("dp", None, "mp"),
            P("dp", None),
            P("dp"),
            P("dp"),
            P("dp"),
            P("dp", None, "mp"),
            P(None, "mp"),
            P("mp", None),
            P("mp", None),
            P(),
            P(),
        ),
        out_specs=(P("dp", None, "mp"), P("dp", "mp"), P("mp", "dp"), P("mp", "dp")),
        check_vma=False,
    )
```

```python
import functools
import math

import jax
import jax.numpy as jnp
from jax import lax
from jax.sharding import PartitionSpec as P

HEADS = 32
KV_HEADS = 4
F32 = jnp.float32
BF16 = jnp.bfloat16


def rms_scale(values, gain):
    inverse = lax.rsqrt(jnp.mean(values * values, axis=-1, keepdims=True) + 1e-06)
    return (values * inverse * gain, inverse)


def rms_back(values, inverse, gain, grad_out):
    scaled = grad_out * gain
    inner = jnp.mean(values * scaled, axis=-1, keepdims=True)
    return inverse * scaled - values * (inverse * inverse * inverse) * inner


def forward_core(query, key_sum, value_sum, query_gain, key_gain):
    scale = 1.0 / math.sqrt(query.shape[-1])
    q_norm, q_inverse = rms_scale(query, query_gain)
    k_norm, k_inverse = rms_scale(key_sum, key_gain)
    q_half = q_norm.astype(jnp.bfloat16)
    k_half = k_norm.astype(jnp.bfloat16)
    v_half = value_sum.astype(jnp.bfloat16)
    score_matrix = (
        jnp.einsum("sqgph,skgh->sgpqk", q_half, k_half, preferred_element_type=jnp.float32) * scale
    )
    length = query.shape[1]
    causal = lax.broadcasted_iota(jnp.int32, (length, length), 0) >= lax.broadcasted_iota(
        jnp.int32, (length, length), 1
    )
    score_matrix = jnp.where(causal, score_matrix, -1e30)
    peak = jnp.max(score_matrix, axis=-1, keepdims=True)
    raised = jnp.exp(score_matrix - peak)
    probs = raised / jnp.sum(raised, axis=-1, keepdims=True)
    p_half = probs.astype(jnp.bfloat16)
    attended = jnp.einsum("sgpqk,skgh->sqgph", p_half, v_half, preferred_element_type=jnp.float32)
    return (attended, (q_inverse, k_inverse, q_half, k_half, v_half, probs, p_half))


def backward_core(d_out, query, key_sum, query_gain, key_gain, saved):
    q_inverse, k_inverse, q_half, k_half, v_half, probs, p_half = saved
    scale = 1.0 / math.sqrt(query.shape[-1])
    out_half = d_out.astype(jnp.bfloat16)
    d_probs = jnp.einsum("sqgph,skgh->sgpqk", out_half, v_half, preferred_element_type=jnp.float32)
    d_value = jnp.einsum("sgpqk,sqgph->skgh", p_half, out_half, preferred_element_type=jnp.float32)
    d_scores = probs * (d_probs - jnp.sum(d_probs * probs, axis=-1, keepdims=True)) * scale
    score_half = d_scores.astype(jnp.bfloat16)
    d_qnorm = jnp.einsum(
        "sgpqk,skgh->sqgph", score_half, k_half, preferred_element_type=jnp.float32
    )
    d_knorm = jnp.einsum(
        "sgpqk,sqgph->skgh", score_half, q_half, preferred_element_type=jnp.float32
    )
    d_query = rms_back(query, q_inverse, query_gain, d_qnorm)
    d_key = rms_back(key_sum, k_inverse, key_gain, d_knorm)
    return (d_query, d_key, d_value)


def attend(query, kv, cot, factor, query_gain, key_gain, length, device_cols):
    tokens = query.shape[0]
    dim = query_gain.shape[0]
    slots = tokens // length
    heads = query.shape[1] // dim
    query = query.reshape(slots, length, 1, heads, dim)
    key = kv[:, :dim].reshape(slots, length, 1, dim)
    value = kv[:, dim:].reshape(slots, length, 1, dim)
    attended, saved = forward_core(query, key, value, query_gain, key_gain)
    d_out = cot.astype(F32).reshape(slots, length, 1, heads, dim)
    d_out = d_out * factor[:, None, None, None, None]
    d_query, d_key, d_value = backward_core(d_out, query, key, query_gain, key_gain, saved)
    pairs = [d_key.reshape(tokens, -1, device_cols), d_value.reshape(tokens, -1, device_cols)]
    d_kv = jnp.stack(pairs, axis=2).reshape(tokens, 2 * dim)
    return (
        attended.reshape(tokens, -1).astype(BF16),
        d_query.reshape(tokens, -1).astype(BF16),
        d_kv.astype(BF16),
    )


def together(*values):
    return lax.optimization_barrier(values)


def pick(array, index):
    return array.at[index].get(mode="promise_in_bounds")


def local(
    n_dp,
    n_mp,
    pool,
    send_table,
    slot_source,
    multiplicity,
    slot_weight,
    cotangent,
    w_query,
    w_key,
    w_value,
    query_gain,
    key_gain,
):
    slots = slot_source.shape[0]
    length = pool.shape[1]
    width = pool.shape[2]
    query_cols = w_query.shape[1]
    key_cols = w_key.shape[1]
    dim = query_gain.shape[0]
    tokens = slots * length
    chips = n_dp // 2
    dp = lax.axis_index("dp")
    mp = lax.axis_index("mp")
    chip, core = dp // 2, dp % 2

    def flip(block, bits):
        return lax.ppermute(block, "dp", [(i, i ^ bits) for i in range(n_dp)])

    def other_chips(blocks):
        return [flip(blocks[k], 2 * k) for k in range(1, chips)]

    def around(blocks):
        return [blocks[0]] + [
            lax.ppermute(blocks[k], "mp", [(i, (i + k) % n_mp) for i in range(n_mp)])
            for k in range(1, n_mp)
        ]

    def up(block, hop):
        return lax.ppermute(block, "mp", [(i, i + 1) for i in range(hop - 1, n_mp - 1)])

    def down(block, hop):
        return lax.ppermute(block, "mp", [(i, i - 1) for i in range(n_mp - hop, 0, -1)])

    outgoing = pick(pool, jnp.maximum(send_table[0], 0))
    outgoing, w_key, w_value = together(outgoing, w_key, w_value)
    arrived = lax.all_to_all(outgoing, "dp", split_axis=0, concat_axis=0, tiled=True)

    share = width // n_dp
    own_key = lax.dynamic_slice_in_dim(w_key, dp * share, share, 0)
    own_value = lax.dynamic_slice_in_dim(w_value, dp * share, share, 0)
    pairs = []
    for head in range(KV_HEADS):
        columns = slice(head * dim, (head + 1) * dim)
        pairs.append(jnp.concatenate([own_key[:, columns], own_value[:, columns]], axis=1))
    pairs = jnp.stack(pairs)
    heads = [(mp + k) % n_mp * KV_HEADS // n_mp for k in range(n_mp)]
    shares = around([lax.dynamic_index_in_dim(pairs, h, 0, False) for h in heads])
    arrived, *shares = together(arrived, *shares)
    shares = jnp.stack(shares)
    rows = pick(arrived, slot_source).reshape(tokens, width)

    ups, downs = [rows], [rows]
    steps = n_mp - 1 if n_mp <= 4 else 1
    near = rows
    for hop in range(1, steps + 1):
        if n_mp <= 4:
            ups.append(up(ups[-1], hop))
            downs.append(down(downs[-1], hop))
        else:
            ups.append(near)
            downs.append(lax.all_gather(near, "mp", axis=0))
        if hop == 1:
            shares = [shares] + other_chips([shares] * chips)
            near, ups[-1], downs[-1], *shares = together(near, ups[-1], downs[-1], *shares)
            shares = jnp.stack(shares)
        elif hop == 2:
            straight = [flip(near, 2 << b) for b in range(chips.bit_length() - 1)]
            other_shares = flip(shares, 1)
            near, ups[-1], downs[-1], other_shares, *straight = together(
                near, ups[-1], downs[-1], other_shares, *straight
            )
    if steps < 2:
        straight = [flip(near, 2 << b) for b in range(chips.bit_length() - 1)]
        other_shares = flip(shares, 1)
    straight = {1 << b: block for b, block in enumerate(straight)}
    plane_rows = [rows] + [
        straight[k] if k in straight else flip(near, 2 * k) for k in range(1, chips)
    ]
    if n_mp <= 4:
        ups[-1], downs[-1], *plane_rows = together(ups[-1], downs[-1], *plane_rows)
    plane_rows = jnp.stack(plane_rows).reshape(chips * tokens, width)

    shares = jnp.stack([shares, other_shares], axis=1).reshape(n_dp, n_mp, share, 2 * dim)
    shares = pick(shares, dp ^ jnp.arange(n_dp))
    w_kv = shares.transpose(1, 0, 2, 3)
    w_kv = w_kv.reshape(n_mp, width, 2 * dim)

    def project(block, index):
        index = jnp.clip(index, 0, n_mp - 1)
        rows_of = lax.dynamic_slice_in_dim(w_query, index * width, width, 0)
        kv_rows = lax.dynamic_index_in_dim(w_kv, (mp - index) % n_mp, 0, False)
        return (
            jnp.dot(block, rows_of, preferred_element_type=F32),
            jnp.dot(block, kv_rows, preferred_element_type=F32),
        )

    if n_mp <= 4:
        terms = [project(rows, mp)]
        for hop in range(1, n_mp):
            if 2 * hop < n_mp:
                terms.append(project(ups[hop], mp - hop))
                terms.append(project(downs[hop], mp + hop))
            else:
                block = jnp.where(mp >= hop, ups[hop], downs[hop])
                terms.append(project(block, jnp.where(mp >= hop, mp - hop, mp + hop)))
        query = sum(term[0] for term in terms)
        kv = sum(term[1] for term in terms)
        blocks = [rows] + [
            jnp.where(mp >= hop, ups[hop], downs[n_mp - hop]) for hop in range(1, n_mp)
        ]
        blocks = jnp.stack(blocks)
        part = lambda k: lax.dynamic_index_in_dim(blocks, (mp - (chip ^ k)) % n_mp, 0, False)
    else:
        x = downs[-1].transpose(1, 0, 2).reshape(tokens, n_mp * width)
        query = jnp.dot(x, w_query, preferred_element_type=F32)
        kv = jnp.dot(
            x,
            pick(w_kv, (mp - jnp.arange(n_mp)) % n_mp).reshape(n_mp * width, 2 * dim),
            preferred_element_type=F32,
        )
        chip_width = n_mp * width // chips
        blocks = x.reshape(tokens, chips, chip_width).transpose(1, 0, 2)
        part = lambda k: lax.dynamic_index_in_dim(blocks, chip ^ k, 0, False)

    chip_rows = [part(k) for k in range(chips)]
    chip_rows = [
        flip(block, 2 * k) if k in straight else block for k, block in enumerate(chip_rows)
    ]
    query, kv, *chip_rows = together(query, kv, *chip_rows)
    chip_rows = [
        block if k in straight or k == 0 else flip(block, 2 * k)
        for k, block in enumerate(chip_rows)
    ]

    factor = multiplicity.astype(F32) * slot_weight / length
    attended, d_query, d_kv = attend(
        query,
        kv,
        cotangent.reshape(tokens, query_cols),
        factor,
        query_gain,
        key_gain,
        length,
        key_cols // n_dp,
    )

    d_query, d_kv, *chip_rows = together(d_query, d_kv, *chip_rows)

    d_all = [flip(d_query, 2 * k) if k in straight else d_query for k in range(chips)]
    spread = around([d_kv] * n_mp)
    *d_all, spread = together(*d_all, jnp.stack(spread))
    d_all = [
        block if k in straight or k == 0 else flip(block, 2 * k) for k, block in enumerate(d_all)
    ]
    d_all = jnp.stack(d_all).reshape(chips * tokens, query_cols)
    chip_rows = jnp.stack(chip_rows).reshape(chips * tokens, -1)
    half = chip_rows.shape[1] // 2

    def query_half(which):
        mine = lax.dynamic_slice_in_dim(chip_rows, which * half, half, 1)
        return jnp.einsum("td,tc->dc", mine, d_all, preferred_element_type=F32)

    other = flip(query_half(1 - core).astype(BF16), 1)
    grad_query = query_half(core) + other.astype(F32)

    if n_mp > KV_HEADS:
        spread = pick(spread, (mp - jnp.arange(n_mp)) % n_mp)
        spread = spread.reshape(KV_HEADS, n_mp // KV_HEADS, tokens, 2 * dim)
        spread = jnp.sum(spread.astype(F32), axis=1).astype(BF16)
        spread_at = lambda index: index
    else:
        spread_at = lambda index: (mp - index) % n_mp
    chip_cols = 2 * key_cols // chips
    if chip_cols != 2 * dim:
        spread = spread.reshape(KV_HEADS, tokens, chips // KV_HEADS, chip_cols)
        spread = spread.transpose(0, 2, 1, 3).reshape(chips, tokens, chip_cols)
    kv_all = [lax.dynamic_index_in_dim(spread, spread_at(chip ^ k), 0, False) for k in range(chips)]
    kv_all = jnp.stack([kv_all[0]] + other_chips(kv_all)).reshape(chips * tokens, chip_cols)
    partial = jnp.einsum("td,tc->dc", plane_rows, kv_all, preferred_element_type=F32)
    mine, theirs = partial[:, : chip_cols // 2], partial[:, chip_cols // 2 :]
    mine, theirs = jnp.where(core == 0, mine, theirs), jnp.where(core == 0, theirs, mine)
    grad_kv = mine + flip(theirs.astype(BF16), 1).astype(F32)
    device_cols = chip_cols // 4

    return (
        attended.reshape(slots, length, query_cols),
        grad_query,
        grad_kv[:, :device_cols],
        grad_kv[:, device_cols:],
    )


def solution(mesh):
    return jax.shard_map(
        functools.partial(local, mesh.shape["dp"], mesh.shape["mp"]),
        mesh=mesh,
        in_specs=(
            P("dp", None, "mp"),
            P("dp", None),
            P("dp"),
            P("dp"),
            P("dp"),
            P("dp", None, "mp"),
            P(None, "mp"),
            P("mp", None),
            P("mp", None),
            P(),
            P(),
        ),
        out_specs=(P("dp", None, "mp"), P("dp", "mp"), P("mp", "dp"), P("mp", "dp")),
        check_vma=False,
    )
```

```python
import functools
import math

import jax
import jax.numpy as jnp
from jax import lax
from jax.sharding import PartitionSpec as P

HEADS = 32
KV_HEADS = 4
F32 = jnp.float32
BF16 = jnp.bfloat16


def rms_scale(values, gain):
    inverse = lax.rsqrt(jnp.mean(values * values, axis=-1, keepdims=True) + 1e-06)
    return (values * inverse * gain, inverse)


def rms_back(values, inverse, gain, grad_out):
    scaled = grad_out * gain
    inner = jnp.mean(values * scaled, axis=-1, keepdims=True)
    return inverse * scaled - values * (inverse * inverse * inverse) * inner


def forward_core(query, key_sum, value_sum, query_gain, key_gain):
    scale = 1.0 / math.sqrt(query.shape[-1])
    q_norm, q_inverse = rms_scale(query, query_gain)
    k_norm, k_inverse = rms_scale(key_sum, key_gain)
    q_half = q_norm.astype(jnp.bfloat16)
    k_half = k_norm.astype(jnp.bfloat16)
    v_half = value_sum.astype(jnp.bfloat16)
    score_matrix = (
        jnp.einsum("sqgph,skgh->sgpqk", q_half, k_half, preferred_element_type=jnp.float32) * scale
    )
    length = query.shape[1]
    causal = lax.broadcasted_iota(jnp.int32, (length, length), 0) >= lax.broadcasted_iota(
        jnp.int32, (length, length), 1
    )
    score_matrix = jnp.where(causal, score_matrix, -1e30)
    peak = jnp.max(score_matrix, axis=-1, keepdims=True)
    raised = jnp.exp(score_matrix - peak)
    probs = raised / jnp.sum(raised, axis=-1, keepdims=True)
    p_half = probs.astype(jnp.bfloat16)
    attended = jnp.einsum("sgpqk,skgh->sqgph", p_half, v_half, preferred_element_type=jnp.float32)
    return (attended, (q_inverse, k_inverse, q_half, k_half, v_half, probs, p_half))


def backward_core(d_out, query, key_sum, query_gain, key_gain, saved):
    q_inverse, k_inverse, q_half, k_half, v_half, probs, p_half = saved
    scale = 1.0 / math.sqrt(query.shape[-1])
    out_half = d_out.astype(jnp.bfloat16)
    d_probs = jnp.einsum("sqgph,skgh->sgpqk", out_half, v_half, preferred_element_type=jnp.float32)
    d_value = jnp.einsum("sgpqk,sqgph->skgh", p_half, out_half, preferred_element_type=jnp.float32)
    d_scores = probs * (d_probs - jnp.sum(d_probs * probs, axis=-1, keepdims=True)) * scale
    score_half = d_scores.astype(jnp.bfloat16)
    d_qnorm = jnp.einsum(
        "sgpqk,skgh->sqgph", score_half, k_half, preferred_element_type=jnp.float32
    )
    d_knorm = jnp.einsum(
        "sgpqk,sqgph->skgh", score_half, q_half, preferred_element_type=jnp.float32
    )
    d_query = rms_back(query, q_inverse, query_gain, d_qnorm)
    d_key = rms_back(key_sum, k_inverse, key_gain, d_knorm)
    return (d_query, d_key, d_value)


def attend(query, kv, cot, factor, query_gain, key_gain, length, device_cols, beside):
    tokens = query.shape[0]
    dim = query_gain.shape[0]
    slots = tokens // length
    heads = query.shape[1] // dim
    query = query.reshape(slots, length, 1, heads, dim)
    key = kv[:, :dim].reshape(slots, length, 1, dim)
    value = kv[:, dim:].reshape(slots, length, 1, dim)
    attended, saved = forward_core(query, key, value, query_gain, key_gain)
    *saved, probs, p_half = saved
    probs, *beside = together(probs, *beside)
    saved = (*saved, probs, p_half)
    d_out = cot.astype(F32).reshape(slots, length, 1, heads, dim)
    d_out = d_out * factor[:, None, None, None, None]
    d_query, d_key, d_value = backward_core(d_out, query, key, query_gain, key_gain, saved)
    pairs = [d_key.reshape(tokens, -1, device_cols), d_value.reshape(tokens, -1, device_cols)]
    d_kv = jnp.stack(pairs, axis=2).reshape(tokens, 2 * dim)
    return (
        attended.reshape(tokens, -1).astype(BF16),
        d_query.reshape(tokens, -1).astype(BF16),
        d_kv.astype(BF16),
        beside,
    )


def together(*values):
    return lax.optimization_barrier(values)


def pick(array, index):
    return array.at[index].get(mode="promise_in_bounds")


def local(
    n_dp,
    n_mp,
    pool,
    send_table,
    slot_source,
    multiplicity,
    slot_weight,
    cotangent,
    w_query,
    w_key,
    w_value,
    query_gain,
    key_gain,
):
    slots = slot_source.shape[0]
    length = pool.shape[1]
    width = pool.shape[2]
    query_cols = w_query.shape[1]
    key_cols = w_key.shape[1]
    dim = query_gain.shape[0]
    tokens = slots * length
    chips = n_dp // 2
    dp = lax.axis_index("dp")
    mp = lax.axis_index("mp")
    chip, core = dp // 2, dp % 2

    def flip(block, bits):
        return lax.ppermute(block, "dp", [(i, i ^ bits) for i in range(n_dp)])

    def other_chips(blocks):
        return [flip(blocks[k], 2 * k) for k in range(1, chips)]

    def around(blocks):
        return [blocks[0]] + [
            lax.ppermute(blocks[k], "mp", [(i, (i + k) % n_mp) for i in range(n_mp)])
            for k in range(1, n_mp)
        ]

    near = [1 << b for b in range(chips.bit_length() - 1)]

    def from_near(block):
        return [flip(block, 2 * k) for k in near]

    def from_far(block, arrived):
        arrived = dict(zip(near, arrived))
        middle = block.shape[0] // 2
        blocks = [block]
        for k in range(1, chips):
            bits = [n for n in near if k & n]
            if len(bits) == 1:
                blocks.append(arrived[k])
            elif len(bits) == 2:
                first = flip(arrived[bits[0]][:middle], 2 * bits[1])
                second = flip(arrived[bits[1]][middle:], 2 * bits[0])
                blocks.append(jnp.concatenate([first, second]))
            else:
                blocks.append(flip(block, 2 * k))
        return blocks

    outgoing = pick(pool, jnp.maximum(send_table[0], 0))
    outgoing, w_key, w_value = together(outgoing, w_key, w_value)
    arrived = lax.all_to_all(outgoing, "dp", split_axis=0, concat_axis=0, tiled=True)

    share = width // n_dp
    own_key = lax.dynamic_slice_in_dim(w_key, dp * share, share, 0)
    own_value = lax.dynamic_slice_in_dim(w_value, dp * share, share, 0)
    pairs = []
    for head in range(KV_HEADS):
        columns = slice(head * dim, (head + 1) * dim)
        pairs.append(jnp.concatenate([own_key[:, columns], own_value[:, columns]], axis=1))
    pairs = jnp.stack(pairs)
    heads = [(mp + k) % n_mp * KV_HEADS // n_mp for k in range(n_mp)]
    shares = around([lax.dynamic_index_in_dim(pairs, h, 0, False) for h in heads])
    arrived, *shares = together(arrived, *shares)
    shares = jnp.stack(shares)
    rows = pick(arrived, slot_source).reshape(tokens, width)

    x = lax.all_gather(rows, "mp", axis=1, tiled=True)
    shares = jnp.stack([shares] + other_chips([shares] * chips))
    native, shares = together(rows, shares)
    other_shares, *plane_rows = together(flip(shares, 1), *from_near(native))
    plane_rows = jnp.stack(from_far(native, plane_rows)).reshape(chips * tokens, width)

    shares = jnp.stack([shares, other_shares], axis=1).reshape(n_dp * n_mp, share, 2 * dim)
    order = (dp ^ jnp.arange(n_dp))[None, :] * n_mp + ((mp - jnp.arange(n_mp)) % n_mp)[:, None]
    w_kv = pick(shares, order.reshape(-1)).reshape(n_mp * width, 2 * dim)

    x, w_kv, plane_rows = together(x, w_kv, plane_rows)
    query = jnp.dot(x, w_query, preferred_element_type=F32)
    kv = jnp.dot(x, w_kv, preferred_element_type=F32)

    chip_width = n_mp * width // chips
    chip_rows = [
        lax.dynamic_slice_in_dim(x, (chip ^ k) * chip_width, chip_width, 1) for k in range(chips)
    ]
    near_rows = [flip(chip_rows[k], 2 * k) for k in near]

    factor = multiplicity.astype(F32) * slot_weight / length
    attended, d_query, d_kv, near_rows = attend(
        query,
        kv,
        cotangent.reshape(tokens, query_cols),
        factor,
        query_gain,
        key_gain,
        length,
        key_cols // n_dp,
        near_rows,
    )

    near_rows = dict(zip(near, near_rows))
    chip_rows = [
        chip_rows[0] if k == 0 else near_rows[k] if k in near else flip(chip_rows[k], 2 * k)
        for k in range(chips)
    ]
    d_query, d_kv, *chip_rows = together(d_query, d_kv, *chip_rows)

    d_near = from_near(d_query)
    spread = around([d_kv] * n_mp)
    spread, *d_near = together(jnp.stack(spread), *d_near)
    d_all = from_far(d_query, d_near)
    half = chip_width // 2
    early = [0] + near
    late = [k for k in range(chips) if k not in early]

    def query_half(which):
        total = 0
        for some in (early, late):
            mine = jnp.concatenate([chip_rows[k] for k in some])
            mine = lax.dynamic_slice_in_dim(mine, which * half, half, 1)
            theirs = jnp.concatenate([d_all[k] for k in some])
            total = total + jnp.einsum("td,tc->dc", mine, theirs, preferred_element_type=F32)
        return total

    other = flip(query_half(1 - core).astype(BF16), 1)
    grad_query = query_half(core) + other.astype(F32)

    if n_mp > KV_HEADS:
        spread = pick(spread, (mp - jnp.arange(n_mp)) % n_mp)
        spread = spread.reshape(KV_HEADS, n_mp // KV_HEADS, tokens, 2 * dim)
        spread = jnp.sum(spread.astype(F32), axis=1).astype(BF16)
        spread_at = lambda index: index
    else:
        spread_at = lambda index: (mp - index) % n_mp
    chip_cols = 2 * key_cols // chips
    if chip_cols != 2 * dim:
        spread = spread.reshape(KV_HEADS, tokens, chips // KV_HEADS, chip_cols)
        spread = spread.transpose(0, 2, 1, 3).reshape(chips, tokens, chip_cols)
    kv_all = [lax.dynamic_index_in_dim(spread, spread_at(chip ^ k), 0, False) for k in range(chips)]
    kv_all = jnp.stack([kv_all[0]] + other_chips(kv_all)).reshape(chips * tokens, chip_cols)
    partial = jnp.einsum("td,tc->dc", plane_rows, kv_all, preferred_element_type=F32)
    mine, theirs = partial[:, : chip_cols // 2], partial[:, chip_cols // 2 :]
    mine, theirs = jnp.where(core == 0, mine, theirs), jnp.where(core == 0, theirs, mine)
    grad_kv = mine + flip(theirs.astype(BF16), 1).astype(F32)
    device_cols = chip_cols // 4

    return (
        attended.reshape(slots, length, query_cols),
        grad_query,
        grad_kv[:, :device_cols],
        grad_kv[:, device_cols:],
    )


def solution(mesh):
    return jax.shard_map(
        functools.partial(local, mesh.shape["dp"], mesh.shape["mp"]),
        mesh=mesh,
        in_specs=(
            P("dp", None, "mp"),
            P("dp", None),
            P("dp"),
            P("dp"),
            P("dp"),
            P("dp", None, "mp"),
            P(None, "mp"),
            P("mp", None),
            P("mp", None),
            P(),
            P(),
        ),
        out_specs=(P("dp", None, "mp"), P("dp", "mp"), P("mp", "dp"), P("mp", "dp")),
        check_vma=False,
    )
```

```python
import functools
import math

import jax
import jax.numpy as jnp
from jax import lax
from jax.experimental import pallas as pl
from jax.experimental.pallas import tpu as pltpu
from jax.sharding import PartitionSpec as P

HEADS = 32
KV_HEADS = 4
F32 = jnp.float32
BF16 = jnp.bfloat16


def dot(a, b, contract):
    return lax.dot_general(a, b, ((contract[0], contract[1]), ((), ())), preferred_element_type=F32)


def rms_back(values, inverse, gain, grad_out):
    scaled = grad_out * gain
    inner = jnp.mean(values * scaled, axis=-1, keepdims=True)
    return inverse * scaled - values * (inverse * inverse * inverse) * inner


def attend_tile(query, key, value, d_out, query_gain, key_gain, length):
    tokens, dim = key.shape
    heads = query.shape[1] // dim
    scale = 1.0 / math.sqrt(dim)

    def stack(wide):
        return jnp.concatenate([wide[:, h * dim : (h + 1) * dim] for h in range(heads)], axis=0)

    def unstack(tall):
        return jnp.concatenate(
            [tall[h * tokens : (h + 1) * tokens] for h in range(heads)], axis=1
        )

    query = stack(query)
    q_inverse = lax.rsqrt(jnp.mean(query * query, axis=-1, keepdims=True) + 1e-06)
    q_half = (query * q_inverse * query_gain).astype(BF16)
    k_inverse = lax.rsqrt(jnp.mean(key * key, axis=-1, keepdims=True) + 1e-06)
    k_half = (key * k_inverse * key_gain).astype(BF16)
    v_half = value.astype(BF16)
    out_half = stack(d_out).astype(BF16)

    shape = (tokens, tokens)
    row = lax.broadcasted_iota(jnp.int32, shape, 0)
    col = lax.broadcasted_iota(jnp.int32, shape, 1)
    size = jnp.full(shape, length, jnp.int32)
    allowed = (row >= col) & (lax.div(row, size) == lax.div(col, size))
    allowed = jnp.concatenate([allowed] * heads, axis=0)

    scores = dot(q_half, k_half, ((1,), (1,))) * scale
    scores = jnp.where(allowed, scores, -1e30)
    raised = jnp.exp(scores - jnp.max(scores, axis=-1, keepdims=True))
    probs = raised / jnp.sum(raised, axis=-1, keepdims=True)
    p_half = probs.astype(BF16)
    attended = dot(p_half, v_half, ((1,), (0,)))
    d_probs = dot(out_half, v_half, ((1,), (1,)))
    d_value = dot(p_half, out_half, ((0,), (0,)))
    inner = jnp.sum(d_probs * probs, axis=-1, keepdims=True)
    score_half = (probs * (d_probs - inner) * scale).astype(BF16)
    d_qnorm = dot(score_half, k_half, ((1,), (0,)))
    d_knorm = dot(score_half, q_half, ((0,), (0,)))
    d_query = rms_back(query, q_inverse, query_gain, d_qnorm)
    d_key = rms_back(key, k_inverse, key_gain, d_knorm)
    return (
        unstack(attended),
        unstack(d_query),
        d_key,
        d_value,
    )


def attend_kernel(
    length,
    device_cols,
    x_ref,
    wq_ref,
    wkv_ref,
    d_out_ref,
    query_gain_ref,
    key_gain_ref,
    attended_ref,
    dq_ref,
    dkv_ref,
    query_ref,
    kv_ref,
):
    step = pl.program_id(0)
    x = x_ref[...]
    query_part = jnp.dot(x, wq_ref[...], preferred_element_type=F32)
    kv_part = jnp.dot(x, wkv_ref[...], preferred_element_type=F32)

    @pl.when(step == 0)
    def _():
        query_ref[...] = query_part
        kv_ref[...] = kv_part

    @pl.when(step > 0)
    def _():
        query_ref[...] += query_part
        kv_ref[...] += kv_part

    @pl.when(step == pl.num_programs(0) - 1)
    def _():
        tokens = query_ref.shape[0]
        dim = query_gain_ref.shape[1]
        tile = min(tokens, max(1, 128 // length) * length)
        for start in range(0, tokens, tile):
            rows = slice(start, start + tile)
            attended, d_query, d_key, d_value = attend_tile(
                query_ref[rows, :],
                kv_ref[rows, :dim],
                kv_ref[rows, dim:],
                d_out_ref[rows, :],
                query_gain_ref[...],
                key_gain_ref[...],
                length,
            )
            attended_ref[rows, :] = attended
            dq_ref[rows, :] = d_query
            for first in range(0, dim, device_cols):
                columns = slice(first, first + device_cols)
                pair = jnp.concatenate([d_key[:, columns], d_value[:, columns]], axis=1)
                dkv_ref[rows, 2 * first : 2 * first + 2 * device_cols] = pair


def attend(x, w_query, w_kv, d_out, query_gain, key_gain, length, device_cols):
    tokens, depth = x.shape
    cols = w_query.shape[1]
    kv_cols = w_kv.shape[1]
    block = depth // 4
    whole = lambda shape: pl.BlockSpec(shape, lambda b: (0, 0))
    return pl.pallas_call(
        functools.partial(attend_kernel, length, device_cols),
        grid=(depth // block,),
        in_specs=[
            pl.BlockSpec((tokens, block), lambda b: (0, b)),
            pl.BlockSpec((block, cols), lambda b: (b, 0)),
            pl.BlockSpec((block, kv_cols), lambda b: (b, 0)),
            whole(d_out.shape),
            whole(query_gain.shape),
            whole(key_gain.shape),
        ],
        out_specs=[whole((tokens, cols)), whole((tokens, cols)), whole((tokens, kv_cols))],
        out_shape=[
            jax.ShapeDtypeStruct((tokens, cols), F32),
            jax.ShapeDtypeStruct((tokens, cols), F32),
            jax.ShapeDtypeStruct((tokens, kv_cols), F32),
        ],
        scratch_shapes=[pltpu.VMEM((tokens, cols), F32), pltpu.VMEM((tokens, kv_cols), F32)],
        compiler_params=pltpu.CompilerParams(vmem_limit_bytes=40 * 1024 * 1024),
        cost_estimate=pl.CostEstimate(
            flops=10 * tokens * depth * (cols + kv_cols),
            bytes_accessed=8 * w_query.size,
            transcendentals=tokens * cols,
        ),
    )(x, w_query, w_kv, d_out, query_gain, key_gain)


def together(*values):
    return lax.optimization_barrier(values)


def pick(array, index):
    return array.at[index].get(mode="promise_in_bounds")


def local(
    n_dp,
    n_mp,
    pool,
    send_table,
    slot_source,
    multiplicity,
    slot_weight,
    cotangent,
    w_query,
    w_key,
    w_value,
    query_gain,
    key_gain,
):
    slots = slot_source.shape[0]
    length = pool.shape[1]
    width = pool.shape[2]
    query_cols = w_query.shape[1]
    key_cols = w_key.shape[1]
    dim = query_gain.shape[0]
    tokens = slots * length
    chips = n_dp // 2
    dp = lax.axis_index("dp")
    mp = lax.axis_index("mp")
    chip, core = dp // 2, dp % 2

    def flip(block, bits):
        return lax.ppermute(block, "dp", [(i, i ^ bits) for i in range(n_dp)])

    def other_chips(blocks):
        return [flip(blocks[k], 2 * k) for k in range(1, chips)]

    def around(blocks):
        return [blocks[0]] + [
            lax.ppermute(blocks[k], "mp", [(i, (i + k) % n_mp) for i in range(n_mp)])
            for k in range(1, n_mp)
        ]

    near = [1 << b for b in range(chips.bit_length() - 1)]

    def from_near(block):
        return [flip(block, 2 * k) for k in near]

    def from_far(block, arrived):
        arrived = dict(zip(near, arrived))
        middle = block.shape[0] // 2
        blocks = [block]
        for k in range(1, chips):
            bits = [n for n in near if k & n]
            if len(bits) == 1:
                blocks.append(arrived[k])
            elif len(bits) == 2:
                first = flip(arrived[bits[0]][:middle], 2 * bits[1])
                second = flip(arrived[bits[1]][middle:], 2 * bits[0])
                blocks.append(jnp.concatenate([first, second]))
            else:
                blocks.append(flip(block, 2 * k))
        return blocks

    outgoing = pick(pool, jnp.maximum(send_table[0], 0))
    outgoing, w_key, w_value = together(outgoing, w_key, w_value)
    arrived = lax.all_to_all(outgoing, "dp", split_axis=0, concat_axis=0, tiled=True)

    share = width // n_dp
    own_key = lax.dynamic_slice_in_dim(w_key, dp * share, share, 0)
    own_value = lax.dynamic_slice_in_dim(w_value, dp * share, share, 0)
    pairs = []
    for head in range(KV_HEADS):
        columns = slice(head * dim, (head + 1) * dim)
        pairs.append(jnp.concatenate([own_key[:, columns], own_value[:, columns]], axis=1))
    pairs = jnp.stack(pairs)
    heads = [(mp + k) % n_mp * KV_HEADS // n_mp for k in range(n_mp)]
    shares = around([lax.dynamic_index_in_dim(pairs, h, 0, False) for h in heads])
    arrived, *shares = together(arrived, *shares)
    shares = jnp.stack(shares)
    rows = pick(arrived, slot_source).reshape(tokens, width)

    x = lax.all_gather(rows, "mp", axis=1, tiled=True)
    shares = jnp.stack([shares] + other_chips([shares] * chips))
    native, shares = together(rows, shares)
    other_shares, *plane_rows = together(flip(shares, 1), *from_near(native))
    plane_rows = jnp.stack(from_far(native, plane_rows)).reshape(chips * tokens, width)

    shares = jnp.stack([shares, other_shares], axis=1).reshape(n_dp * n_mp, share, 2 * dim)
    order = (dp ^ jnp.arange(n_dp))[None, :] * n_mp + ((mp - jnp.arange(n_mp)) % n_mp)[:, None]
    w_kv = pick(shares, order.reshape(-1)).reshape(n_mp * width, 2 * dim)

    x, w_kv, plane_rows = together(x, w_kv, plane_rows)

    chip_width = n_mp * width // chips
    chip_rows = [
        lax.dynamic_slice_in_dim(x, (chip ^ k) * chip_width, chip_width, 1) for k in range(chips)
    ]
    x, *chip_rows = together(x, *chip_rows)
    chip_rows = [chip_rows[0]] + other_chips(chip_rows)

    factor = multiplicity.astype(F32) * slot_weight / length
    d_out = (cotangent.astype(F32) * factor[:, None, None]).astype(BF16).astype(F32)
    attended, d_query, d_kv = attend(
        x,
        w_query,
        w_kv,
        d_out.reshape(tokens, query_cols),
        query_gain[None, :],
        key_gain[None, :],
        length,
        key_cols // n_dp,
    )
    attended, d_query, d_kv = [value.astype(BF16) for value in (attended, d_query, d_kv)]
    d_query, d_kv, *chip_rows = together(d_query, d_kv, *chip_rows)

    d_all = [d_query] + other_chips([d_query] * chips)
    spread = jnp.stack(around([d_kv] * n_mp))
    half = chip_width // 2
    early = [0] + near
    late = [k for k in range(chips) if k not in early]

    def product(some, which):
        mine = jnp.concatenate([chip_rows[k] for k in some])
        mine = lax.dynamic_slice_in_dim(mine, which * half, half, 1)
        theirs = jnp.concatenate([d_all[k] for k in some])
        return jnp.einsum("td,tc->dc", mine, theirs, preferred_element_type=F32)

    other = flip((product(early, 1 - core) + product(late, 1 - core)).astype(BF16), 1)
    grad_query = product(late, core) + (product(early, core) + other.astype(F32))

    if n_mp > KV_HEADS:
        spread = pick(spread, (mp - jnp.arange(n_mp)) % n_mp)
        spread = spread.reshape(KV_HEADS, n_mp // KV_HEADS, tokens, 2 * dim)
        spread = jnp.sum(spread.astype(F32), axis=1).astype(BF16)
        spread_at = lambda index: index
    else:
        spread_at = lambda index: (mp - index) % n_mp
    chip_cols = 2 * key_cols // chips
    if chip_cols != 2 * dim:
        spread = spread.reshape(KV_HEADS, tokens, chips // KV_HEADS, chip_cols)
        spread = spread.transpose(0, 2, 1, 3).reshape(chips, tokens, chip_cols)
    kv_all = [lax.dynamic_index_in_dim(spread, spread_at(chip ^ k), 0, False) for k in range(chips)]
    kv_all = jnp.stack([kv_all[0]] + other_chips(kv_all)).reshape(chips * tokens, chip_cols)
    partial = jnp.einsum("td,tc->dc", plane_rows, kv_all, preferred_element_type=F32)
    mine, theirs = partial[:, : chip_cols // 2], partial[:, chip_cols // 2 :]
    mine, theirs = jnp.where(core == 0, mine, theirs), jnp.where(core == 0, theirs, mine)
    grad_kv = mine + flip(theirs.astype(BF16), 1).astype(F32)
    device_cols = chip_cols // 4

    return (
        attended.reshape(slots, length, query_cols),
        grad_query,
        grad_kv[:, :device_cols],
        grad_kv[:, device_cols:],
    )


def solution(mesh):
    return jax.shard_map(
        functools.partial(local, mesh.shape["dp"], mesh.shape["mp"]),
        mesh=mesh,
        in_specs=(
            P("dp", None, "mp"),
            P("dp", None),
            P("dp"),
            P("dp"),
            P("dp"),
            P("dp", None, "mp"),
            P(None, "mp"),
            P("mp", None),
            P("mp", None),
            P(),
            P(),
        ),
        out_specs=(P("dp", None, "mp"), P("dp", "mp"), P("mp", "dp"), P("mp", "dp")),
        check_vma=False,
    )
```

```python
import functools
import math

import jax
import jax.numpy as jnp
from jax import lax
from jax.experimental import pallas as pl
from jax.experimental.pallas import tpu as pltpu
from jax.sharding import PartitionSpec as P

HEADS = 32
KV_HEADS = 4
F32 = jnp.float32
BF16 = jnp.bfloat16


def dot(a, b, contract):
    return lax.dot_general(a, b, ((contract[0], contract[1]), ((), ())), preferred_element_type=F32)


def rms_back(values, inverse, gain, grad_out):
    scaled = grad_out * gain
    inner = jnp.mean(values * scaled, axis=-1, keepdims=True)
    return inverse * scaled - values * (inverse * inverse * inverse) * inner


def attend_tile(query, key, value, d_out, query_gain, key_gain, length):
    tokens, dim = key.shape
    heads = query.shape[1] // dim
    scale = 1.0 / math.sqrt(dim)

    def stack(wide):
        return jnp.concatenate([wide[:, h * dim : (h + 1) * dim] for h in range(heads)], axis=0)

    def unstack(tall):
        return jnp.concatenate(
            [tall[h * tokens : (h + 1) * tokens] for h in range(heads)], axis=1
        )

    query = stack(query)
    q_inverse = lax.rsqrt(jnp.mean(query * query, axis=-1, keepdims=True) + 1e-06)
    q_half = (query * q_inverse * query_gain).astype(BF16)
    k_inverse = lax.rsqrt(jnp.mean(key * key, axis=-1, keepdims=True) + 1e-06)
    k_half = (key * k_inverse * key_gain).astype(BF16)
    v_half = value.astype(BF16)
    out_half = stack(d_out).astype(BF16)

    shape = (tokens, tokens)
    row = lax.broadcasted_iota(jnp.int32, shape, 0)
    col = lax.broadcasted_iota(jnp.int32, shape, 1)
    size = jnp.full(shape, length, jnp.int32)
    allowed = (row >= col) & (lax.div(row, size) == lax.div(col, size))
    allowed = jnp.concatenate([allowed] * heads, axis=0)

    scores = dot(q_half, k_half, ((1,), (1,))) * scale
    scores = jnp.where(allowed, scores, -1e30)
    raised = jnp.exp(scores - jnp.max(scores, axis=-1, keepdims=True))
    probs = raised / jnp.sum(raised, axis=-1, keepdims=True)
    p_half = probs.astype(BF16)
    attended = dot(p_half, v_half, ((1,), (0,)))
    d_probs = dot(out_half, v_half, ((1,), (1,)))
    d_value = dot(p_half, out_half, ((0,), (0,)))
    inner = jnp.sum(d_probs * probs, axis=-1, keepdims=True)
    score_half = (probs * (d_probs - inner) * scale).astype(BF16)
    d_qnorm = dot(score_half, k_half, ((1,), (0,)))
    d_knorm = dot(score_half, q_half, ((0,), (0,)))
    d_query = rms_back(query, q_inverse, query_gain, d_qnorm)
    d_key = rms_back(key, k_inverse, key_gain, d_knorm)
    return (
        unstack(attended),
        unstack(d_query),
        d_key,
        d_value,
    )


def attend_kernel(
    length,
    device_cols,
    x_ref,
    wq_ref,
    wkv_ref,
    d_out_ref,
    query_gain_ref,
    key_gain_ref,
    attended_ref,
    dq_ref,
    dkv_ref,
    query_ref,
    kv_ref,
):
    step = pl.program_id(0)
    x = x_ref[0]
    query_part = jnp.dot(x, wq_ref[...], preferred_element_type=F32)
    kv_part = jnp.dot(x, wkv_ref[...], preferred_element_type=F32)

    @pl.when(step == 0)
    def _():
        query_ref[...] = query_part
        kv_ref[...] = kv_part

    @pl.when(step > 0)
    def _():
        query_ref[...] += query_part
        kv_ref[...] += kv_part

    @pl.when(step == pl.num_programs(0) - 1)
    def _():
        tokens = query_ref.shape[0]
        dim = query_gain_ref.shape[1]
        tile = min(tokens, max(1, 128 // length) * length)
        for start in range(0, tokens, tile):
            rows = slice(start, start + tile)
            attended, d_query, d_key, d_value = attend_tile(
                query_ref[rows, :],
                kv_ref[rows, :dim],
                kv_ref[rows, dim:],
                d_out_ref[rows, :],
                query_gain_ref[...],
                key_gain_ref[...],
                length,
            )
            attended_ref[rows, :] = attended
            dq_ref[rows, :] = d_query
            for first in range(0, dim, device_cols):
                columns = slice(first, first + device_cols)
                pair = jnp.concatenate([d_key[:, columns], d_value[:, columns]], axis=1)
                dkv_ref[rows, 2 * first : 2 * first + 2 * device_cols] = pair


def attend(x, w_query, w_kv, d_out, query_gain, key_gain, length, device_cols):
    blocks, tokens, width = x.shape
    cols = w_query.shape[1]
    kv_cols = w_kv.shape[1]
    whole = lambda shape: pl.BlockSpec(shape, lambda b: (0, 0))
    return pl.pallas_call(
        functools.partial(attend_kernel, length, device_cols),
        grid=(blocks,),
        in_specs=[
            pl.BlockSpec((1, tokens, width), lambda b: (b, 0, 0)),
            pl.BlockSpec((width, cols), lambda b: (b, 0)),
            pl.BlockSpec((width, kv_cols), lambda b: (b, 0)),
            whole(d_out.shape),
            whole(query_gain.shape),
            whole(key_gain.shape),
        ],
        out_specs=[whole((tokens, cols)), whole((tokens, cols)), whole((tokens, kv_cols))],
        out_shape=[
            jax.ShapeDtypeStruct((tokens, cols), F32),
            jax.ShapeDtypeStruct((tokens, cols), F32),
            jax.ShapeDtypeStruct((tokens, kv_cols), F32),
        ],
        scratch_shapes=[pltpu.VMEM((tokens, cols), F32), pltpu.VMEM((tokens, kv_cols), F32)],
        compiler_params=pltpu.CompilerParams(vmem_limit_bytes=40 * 1024 * 1024),
        cost_estimate=pl.CostEstimate(
            flops=20 * x.size * (cols + kv_cols),
            bytes_accessed=8 * w_query.size,
            transcendentals=tokens * cols,
        ),
    )(x, w_query, w_kv, d_out, query_gain, key_gain)


def together(*values):
    return lax.optimization_barrier(values)


def pick(array, index):
    return array.at[index].get(mode="promise_in_bounds")


def local(
    n_dp,
    n_mp,
    pool,
    send_table,
    slot_source,
    multiplicity,
    slot_weight,
    cotangent,
    w_query,
    w_key,
    w_value,
    query_gain,
    key_gain,
):
    slots = slot_source.shape[0]
    length = pool.shape[1]
    width = pool.shape[2]
    query_cols = w_query.shape[1]
    key_cols = w_key.shape[1]
    dim = query_gain.shape[0]
    tokens = slots * length
    chips = n_dp // 2
    dp = lax.axis_index("dp")
    mp = lax.axis_index("mp")
    chip, core = dp // 2, dp % 2

    def flip(block, bits):
        return lax.ppermute(block, "dp", [(i, i ^ bits) for i in range(n_dp)])

    def other_chips(blocks):
        return [flip(blocks[k], 2 * k) for k in range(1, chips)]

    def around(blocks):
        return [blocks[0]] + [
            lax.ppermute(blocks[k], "mp", [(i, (i + k) % n_mp) for i in range(n_mp)])
            for k in range(1, n_mp)
        ]

    near = [1 << b for b in range(chips.bit_length() - 1)]

    def from_near(block):
        return [flip(block, 2 * k) for k in near]

    def from_far(block, arrived):
        arrived = dict(zip(near, arrived))
        middle = block.shape[0] // 2
        pieces = [[block]]
        for k in range(1, chips):
            bits = [n for n in near if k & n]
            if len(bits) == 1:
                pieces.append([arrived[k]])
            elif len(bits) == 2:
                first = flip(arrived[bits[0]][:middle], 2 * bits[1])
                second = flip(arrived[bits[1]][middle:], 2 * bits[0])
                pieces.append([first, second])
            else:
                pieces.append([flip(block, 2 * k)])
        return pieces

    outgoing = pick(pool, jnp.maximum(send_table[0], 0))
    outgoing, w_key, w_value = together(outgoing, w_key, w_value)
    arrived = lax.all_to_all(outgoing, "dp", split_axis=0, concat_axis=0, tiled=True)

    share = width // n_dp
    own_key = lax.dynamic_slice_in_dim(w_key, dp * share, share, 0)
    own_value = lax.dynamic_slice_in_dim(w_value, dp * share, share, 0)
    pairs = []
    for head in range(KV_HEADS):
        columns = slice(head * dim, (head + 1) * dim)
        pairs.append(jnp.concatenate([own_key[:, columns], own_value[:, columns]], axis=1))
    pairs = jnp.stack(pairs)
    heads = [(mp + k) % n_mp * KV_HEADS // n_mp for k in range(n_mp)]
    shares = around([lax.dynamic_index_in_dim(pairs, h, 0, False) for h in heads])
    shares = jnp.stack(shares)
    rows = pick(arrived, slot_source).reshape(tokens, width)

    middle = tokens // 2
    first_rows, second_rows = rows[:middle], rows[middle:]
    x_first = lax.all_gather(first_rows, "mp", axis=0)
    shares = jnp.stack([shares] + other_chips([shares] * chips))
    native, second_rows, shares = together(rows, second_rows, shares)
    x_second = lax.all_gather(second_rows, "mp", axis=0)
    other_shares = flip(shares, 1)
    plane_rows = together(*from_near(native))
    plane_rows = from_far(native, plane_rows)

    shares = jnp.stack([shares, other_shares], axis=1).reshape(n_dp * n_mp, share, 2 * dim)
    order = (dp ^ jnp.arange(n_dp))[None, :] * n_mp + ((mp - jnp.arange(n_mp)) % n_mp)[:, None]
    w_kv = pick(shares, order.reshape(-1)).reshape(n_mp * width, 2 * dim)

    factor = multiplicity.astype(F32) * slot_weight / length
    d_out = (cotangent.astype(F32) * factor[:, None, None]).astype(BF16).astype(F32)
    d_out = d_out.reshape(tokens, query_cols)
    chip_width = n_mp * width // chips

    def chip_part(x, k):
        if chip_width == width:
            return lax.dynamic_index_in_dim(x, chip ^ k, 0, False)
        flat = x.transpose(1, 0, 2).reshape(x.shape[1], -1)
        return lax.dynamic_slice_in_dim(flat, (chip ^ k) * chip_width, chip_width, 1)

    def half_step(x, d_out, beside):
        x, *parts = together(x, *[chip_part(x, k) for k in range(chips)])
        near_parts = [flip(parts[k], 2 * k) for k in near]
        attended, d_query, d_kv = attend(
            x, w_query, w_kv, d_out, query_gain[None, :], key_gain[None, :], length, key_cols // n_dp
        )
        d_query, d_kv, near_parts, beside = lax.optimization_barrier(
            (d_query.astype(BF16), d_kv.astype(BF16), near_parts, beside)
        )
        near_parts = dict(zip(near, near_parts))
        for k in range(1, chips):
            parts[k] = near_parts[k] if k in near_parts else flip(parts[k], 2 * k)
        d_query, *parts = together(d_query, *parts)
        return attended.astype(BF16), d_query, d_kv, parts, beside

    (x_first, *native_near) = together(x_first, *[plane_rows[k][0] for k in near])
    for k, block in zip(near, native_near):
        plane_rows[k] = [block]
    attended, d_query, d_kv, first_parts, plane_rows = half_step(
        x_first, d_out[:middle], plane_rows
    )
    first_all = [d_query] + other_chips([d_query] * chips)

    half = chip_width // 2

    def product(mine, theirs, which):
        mine = lax.dynamic_slice_in_dim(jnp.concatenate(mine), which * half, half, 1)
        return jnp.einsum("td,tc->dc", mine, jnp.concatenate(theirs), preferred_element_type=F32)

    x_second, first_other, first_own = together(
        x_second, product(first_parts, first_all, 1 - core), product(first_parts, first_all, core)
    )
    attended_second, d_query, d_kv_second, second_parts, _ = half_step(x_second, d_out[middle:], [])
    second_all = [d_query] + other_chips([d_query] * chips)
    attended = jnp.concatenate([attended, attended_second])
    d_kv = jnp.concatenate([d_kv, d_kv_second])
    spread = jnp.stack(around([d_kv] * n_mp))
    spread, *second_near = together(spread, *[second_all[k] for k in near])
    for k, block in zip(near, second_near):
        second_all[k] = block

    some = [0] + near
    rest = [k for k in range(chips) if k not in some]

    def second(which):
        return [
            product([second_parts[k] for k in ks], [second_all[k] for k in ks], which)
            for ks in (some, rest)
        ]

    early, late = second(1 - core)
    other = flip((late + (early + first_other)).astype(BF16), 1)
    early, late = second(core)
    grad_query = late + ((early + first_own) + other.astype(F32))

    if n_mp > KV_HEADS:
        spread = pick(spread, (mp - jnp.arange(n_mp)) % n_mp)
        spread = spread.reshape(KV_HEADS, n_mp // KV_HEADS, tokens, 2 * dim)
        spread = jnp.sum(spread.astype(F32), axis=1).astype(BF16)
        spread_at = lambda index: index
    else:
        spread_at = lambda index: (mp - index) % n_mp
    chip_cols = 2 * key_cols // chips
    if chip_cols != 2 * dim:
        spread = spread.reshape(KV_HEADS, tokens, chips // KV_HEADS, chip_cols)
        spread = spread.transpose(0, 2, 1, 3).reshape(chips, tokens, chip_cols)
    kv_all = [lax.dynamic_index_in_dim(spread, spread_at(chip ^ k), 0, False) for k in range(chips)]
    kv_all = [kv_all[0]] + other_chips(kv_all)
    partial = 0
    for pieces, columns in zip(plane_rows, kv_all):
        size = tokens // len(pieces)
        for i, piece in enumerate(pieces):
            part = columns[i * size : (i + 1) * size]
            partial = partial + jnp.einsum("td,tc->dc", piece, part, preferred_element_type=F32)
    mine, theirs = partial[:, : chip_cols // 2], partial[:, chip_cols // 2 :]
    mine, theirs = jnp.where(core == 0, mine, theirs), jnp.where(core == 0, theirs, mine)
    grad_kv = mine + flip(theirs.astype(BF16), 1).astype(F32)
    device_cols = chip_cols // 4

    return (
        attended.reshape(slots, length, query_cols),
        grad_query,
        grad_kv[:, :device_cols],
        grad_kv[:, device_cols:],
    )


def solution(mesh):
    return jax.shard_map(
        functools.partial(local, mesh.shape["dp"], mesh.shape["mp"]),
        mesh=mesh,
        in_specs=(
            P("dp", None, "mp"),
            P("dp", None),
            P("dp"),
            P("dp"),
            P("dp"),
            P("dp", None, "mp"),
            P(None, "mp"),
            P("mp", None),
            P("mp", None),
            P(),
            P(),
        ),
        out_specs=(P("dp", None, "mp"), P("dp", "mp"), P("mp", "dp"), P("mp", "dp")),
        check_vma=False,
    )
```

```python
import functools
import math

import jax
import jax.numpy as jnp
from jax import lax
from jax.experimental import pallas as pl
from jax.experimental.pallas import tpu as pltpu
from jax.sharding import PartitionSpec as P

HEADS = 32
KV_HEADS = 4
F32 = jnp.float32
BF16 = jnp.bfloat16


def dot(a, b, contract):
    return lax.dot_general(a, b, ((contract[0], contract[1]), ((), ())), preferred_element_type=F32)


def rms_back(values, inverse, gain, grad_out):
    scaled = grad_out * gain
    inner = jnp.mean(values * scaled, axis=-1, keepdims=True)
    return inverse * scaled - values * (inverse * inverse * inverse) * inner


def attend_tile(query, key, value, d_out, query_gain, key_gain, length):
    tokens, dim = key.shape
    heads = query.shape[1] // dim
    scale = 1.0 / math.sqrt(dim)

    def stack(wide):
        return jnp.concatenate([wide[:, h * dim : (h + 1) * dim] for h in range(heads)], axis=0)

    def unstack(tall):
        return jnp.concatenate(
            [tall[h * tokens : (h + 1) * tokens] for h in range(heads)], axis=1
        )

    query = stack(query)
    q_inverse = lax.rsqrt(jnp.mean(query * query, axis=-1, keepdims=True) + 1e-06)
    q_half = (query * q_inverse * query_gain).astype(BF16)
    k_inverse = lax.rsqrt(jnp.mean(key * key, axis=-1, keepdims=True) + 1e-06)
    k_half = (key * k_inverse * key_gain).astype(BF16)
    v_half = value.astype(BF16)
    out_half = stack(d_out).astype(BF16)

    shape = (tokens, tokens)
    row = lax.broadcasted_iota(jnp.int32, shape, 0)
    col = lax.broadcasted_iota(jnp.int32, shape, 1)
    size = jnp.full(shape, length, jnp.int32)
    allowed = (row >= col) & (lax.div(row, size) == lax.div(col, size))
    allowed = jnp.concatenate([allowed] * heads, axis=0)

    scores = dot(q_half, k_half, ((1,), (1,))) * scale
    scores = jnp.where(allowed, scores, -1e30)
    raised = jnp.exp(scores - jnp.max(scores, axis=-1, keepdims=True))
    probs = raised / jnp.sum(raised, axis=-1, keepdims=True)
    p_half = probs.astype(BF16)
    attended = dot(p_half, v_half, ((1,), (0,)))
    d_probs = dot(out_half, v_half, ((1,), (1,)))
    d_value = dot(p_half, out_half, ((0,), (0,)))
    inner = jnp.sum(d_probs * probs, axis=-1, keepdims=True)
    score_half = (probs * (d_probs - inner) * scale).astype(BF16)
    d_qnorm = dot(score_half, k_half, ((1,), (0,)))
    d_knorm = dot(score_half, q_half, ((0,), (0,)))
    d_query = rms_back(query, q_inverse, query_gain, d_qnorm)
    d_key = rms_back(key, k_inverse, key_gain, d_knorm)
    return (
        unstack(attended),
        unstack(d_query),
        d_key,
        d_value,
    )


def attend_kernel(
    length,
    device_cols,
    x_ref,
    wq_ref,
    wkv_ref,
    d_out_ref,
    query_gain_ref,
    key_gain_ref,
    attended_ref,
    dq_ref,
    dkv_ref,
    query_ref,
    kv_ref,
):
    step = pl.program_id(0)
    x = x_ref[0]
    query_part = jnp.dot(x, wq_ref[...], preferred_element_type=F32)
    kv_part = jnp.dot(x, wkv_ref[...], preferred_element_type=F32)

    @pl.when(step == 0)
    def _():
        query_ref[...] = query_part
        kv_ref[...] = kv_part

    @pl.when(step > 0)
    def _():
        query_ref[...] += query_part
        kv_ref[...] += kv_part

    @pl.when(step == pl.num_programs(0) - 1)
    def _():
        tokens = query_ref.shape[0]
        dim = query_gain_ref.shape[1]
        tile = min(tokens, max(1, 128 // length) * length)
        for start in range(0, tokens, tile):
            rows = slice(start, start + tile)
            attended, d_query, d_key, d_value = attend_tile(
                query_ref[rows, :],
                kv_ref[rows, :dim],
                kv_ref[rows, dim:],
                d_out_ref[rows, :],
                query_gain_ref[...],
                key_gain_ref[...],
                length,
            )
            attended_ref[rows, :] = attended
            dq_ref[rows, :] = d_query
            for first in range(0, dim, device_cols):
                columns = slice(first, first + device_cols)
                pair = jnp.concatenate([d_key[:, columns], d_value[:, columns]], axis=1)
                dkv_ref[rows, 2 * first : 2 * first + 2 * device_cols] = pair


def attend(x, w_query, w_kv, d_out, query_gain, key_gain, length, device_cols):
    blocks, tokens, width = x.shape
    cols = w_query.shape[1]
    kv_cols = w_kv.shape[1]
    whole = lambda shape: pl.BlockSpec(shape, lambda b: (0, 0))
    return pl.pallas_call(
        functools.partial(attend_kernel, length, device_cols),
        grid=(blocks,),
        in_specs=[
            pl.BlockSpec((1, tokens, width), lambda b: (b, 0, 0)),
            pl.BlockSpec((width, cols), lambda b: (b, 0)),
            pl.BlockSpec((width, kv_cols), lambda b: (b, 0)),
            whole(d_out.shape),
            whole(query_gain.shape),
            whole(key_gain.shape),
        ],
        out_specs=[whole((tokens, cols)), whole((tokens, cols)), whole((tokens, kv_cols))],
        out_shape=[
            jax.ShapeDtypeStruct((tokens, cols), F32),
            jax.ShapeDtypeStruct((tokens, cols), F32),
            jax.ShapeDtypeStruct((tokens, kv_cols), F32),
        ],
        scratch_shapes=[pltpu.VMEM((tokens, cols), F32), pltpu.VMEM((tokens, kv_cols), F32)],
        compiler_params=pltpu.CompilerParams(vmem_limit_bytes=40 * 1024 * 1024),
        cost_estimate=pl.CostEstimate(
            flops=2 * x.size * (cols + kv_cols),
            bytes_accessed=2 * w_query.size,
            transcendentals=tokens * cols,
        ),
    )(x, w_query, w_kv, d_out, query_gain, key_gain)


def together(*values):
    return lax.optimization_barrier(values)


def pick(array, index):
    return array.at[index].get(mode="promise_in_bounds")


def local(
    n_dp,
    n_mp,
    pool,
    send_table,
    slot_source,
    multiplicity,
    slot_weight,
    cotangent,
    w_query,
    w_key,
    w_value,
    query_gain,
    key_gain,
):
    slots = slot_source.shape[0]
    length = pool.shape[1]
    width = pool.shape[2]
    query_cols = w_query.shape[1]
    key_cols = w_key.shape[1]
    dim = query_gain.shape[0]
    tokens = slots * length
    chips = n_dp // 2
    dp = lax.axis_index("dp")
    mp = lax.axis_index("mp")
    chip, core = dp // 2, dp % 2

    def flip(block, bits):
        return lax.ppermute(block, "dp", [(i, i ^ bits) for i in range(n_dp)])

    def other_chips(blocks):
        return [flip(blocks[k], 2 * k) for k in range(1, chips)]

    def around(blocks):
        return [blocks[0]] + [
            lax.ppermute(blocks[k], "mp", [(i, (i + k) % n_mp) for i in range(n_mp)])
            for k in range(1, n_mp)
        ]

    near = [1 << b for b in range(chips.bit_length() - 1)]

    def from_near(block):
        return [flip(block, 2 * k) for k in near]

    def from_far(block, arrived):
        arrived = dict(zip(near, arrived))
        middle = block.shape[0] // 2
        pieces = [[block]]
        for k in range(1, chips):
            bits = [n for n in near if k & n]
            if len(bits) == 1:
                pieces.append([arrived[k]])
            elif len(bits) == 2:
                first = flip(arrived[bits[0]][:middle], 2 * bits[1])
                second = flip(arrived[bits[1]][middle:], 2 * bits[0])
                pieces.append([first, second])
            else:
                pieces.append([flip(block, 2 * k)])
        return pieces

    outgoing = pick(pool, jnp.maximum(send_table[0], 0))
    outgoing, w_key, w_value = together(outgoing, w_key, w_value)
    arrived = lax.all_to_all(outgoing, "dp", split_axis=0, concat_axis=0, tiled=True)

    axes = len(near)
    share = width // axes // 4
    own = [
        b * (width // axes) + ((chip >> b) % 2 * 2 + core) * share for b in range(axes)
    ]
    own_key = jnp.concatenate([lax.dynamic_slice_in_dim(w_key, i, share, 0) for i in own])
    own_value = jnp.concatenate([lax.dynamic_slice_in_dim(w_value, i, share, 0) for i in own])
    pairs = []
    for head in range(KV_HEADS):
        columns = slice(head * dim, (head + 1) * dim)
        pairs.append(jnp.concatenate([own_key[:, columns], own_value[:, columns]], axis=1))
    pairs = jnp.stack(pairs)
    heads = [(mp + k) % n_mp * KV_HEADS // n_mp for k in range(n_mp)]
    pairs = [lax.dynamic_index_in_dim(pairs, h, 0, False) for h in heads]
    rows = pick(arrived, slot_source).reshape(tokens, width)
    rows, pairs = lax.optimization_barrier((rows, pairs))
    shares = around(pairs)
    shares = jnp.stack(shares).reshape(n_mp, axes, share, 2 * dim)
    shares = [shares[:, b] for b in range(axes)]

    middle = tokens // 2
    first_rows, second_rows = rows[:middle], rows[middle:]
    x_first = lax.all_gather(first_rows, "mp", axis=0)
    other_shares = [flip(block, 2 * k) for k, block in zip(near, shares)]
    native, second_rows, other_shares = lax.optimization_barrier((rows, second_rows, other_shares))
    x_second = lax.all_gather(second_rows, "mp", axis=0)
    shares = jnp.stack([block for pair in zip(shares, other_shares) for block in pair])
    shares = jnp.stack([shares, flip(shares, 1)]).reshape(-1, share, 2 * dim)

    places = []
    for i in range(n_mp):
        for b in range(axes):
            for bit in range(2):
                for c in range(2):
                    place = ((c ^ core) * axes + b) * 2 + (bit ^ (chip >> b) % 2)
                    places.append(place * n_mp + (mp - i) % n_mp)
    w_kv = pick(shares, jnp.stack(places)).reshape(n_mp * width, 2 * dim)
    w_kv, *plane_rows = together(w_kv, *from_near(native))
    plane_rows = from_far(native, plane_rows)

    factor = multiplicity.astype(F32) * slot_weight / length
    d_out = (cotangent.astype(F32) * factor[:, None, None]).astype(BF16).astype(F32)
    d_out = d_out.reshape(tokens, query_cols)
    chip_width = n_mp * width // chips

    def chip_part(x, k):
        if chip_width == width:
            return lax.dynamic_index_in_dim(x, chip ^ k, 0, False)
        flat = x.transpose(1, 0, 2).reshape(x.shape[1], -1)
        return lax.dynamic_slice_in_dim(flat, (chip ^ k) * chip_width, chip_width, 1)

    def half_step(x, d_out, before, beside):
        x, *parts = together(x, *[chip_part(x, k) for k in range(chips)])
        near_parts = [flip(parts[k], 2 * k) for k in near]
        x, before = lax.optimization_barrier((x, before))
        attended, d_query, d_kv = attend(
            x, w_query, w_kv, d_out, query_gain[None, :], key_gain[None, :], length, key_cols // n_dp
        )
        d_query, d_kv, near_parts, beside = lax.optimization_barrier(
            (d_query.astype(BF16), d_kv.astype(BF16), near_parts, beside)
        )
        near_parts = dict(zip(near, near_parts))
        for k in range(1, chips):
            parts[k] = near_parts[k] if k in near_parts else flip(parts[k], 2 * k)
        return attended.astype(BF16), d_query, d_kv, parts, before, beside

    x_first, *native_near = together(x_first, *[plane_rows[k][0] for k in near])
    for k, block in zip(near, native_near):
        plane_rows[k] = [block]
    attended, d_query, d_kv, first_parts, _, plane_rows = half_step(
        x_first, d_out[:middle], [], plane_rows
    )
    d_query, *first_parts = together(d_query, *first_parts)
    first_all = [d_query] + other_chips([d_query] * chips)

    half = chip_width // 2

    def product(mine, theirs, which):
        mine = lax.dynamic_slice_in_dim(jnp.concatenate(mine), which * half, half, 1)
        return jnp.einsum("td,tc->dc", mine, jnp.concatenate(theirs), preferred_element_type=F32)

    x_second, *first_near = together(x_second, *[first_all[k] for k in near])
    for k, block in zip(near, first_near):
        first_all[k] = block
    products = [product(first_parts, first_all, which) for which in (1 - core, core)]
    attended_second, d_query, d_kv_second, second_parts, products, _ = half_step(
        x_second, d_out[middle:], products, []
    )
    first_other, first_own = products
    attended = jnp.concatenate([attended, attended_second])
    d_kv = jnp.concatenate([d_kv, d_kv_second])
    spread = around([d_kv] * n_mp)
    d_query, spread, second_parts = lax.optimization_barrier((d_query, spread, second_parts))
    spread = jnp.stack(spread)
    second_all = [d_query] + other_chips([d_query] * chips)

    if n_mp > KV_HEADS:
        spread = pick(spread, (mp - jnp.arange(n_mp)) % n_mp)
        spread = spread.reshape(KV_HEADS, n_mp // KV_HEADS, tokens, 2 * dim)
        spread = jnp.sum(spread.astype(F32), axis=1).astype(BF16)
        spread_at = lambda index: index
    else:
        spread_at = lambda index: (mp - index) % n_mp
    chip_cols = 2 * key_cols // chips
    if chip_cols != 2 * dim:
        spread = spread.reshape(KV_HEADS, tokens, chips // KV_HEADS, chip_cols)
        spread = spread.transpose(0, 2, 1, 3).reshape(chips, tokens, chip_cols)
    kv_all = [lax.dynamic_index_in_dim(spread, spread_at(chip ^ k), 0, False) for k in range(chips)]
    kv_all = [kv_all[0]] + other_chips(kv_all)
    second_near = [second_all[k] for k in near]
    kv_all, second_near = lax.optimization_barrier((kv_all, second_near))
    for k, block in zip(near, second_near):
        second_all[k] = block
    some = [0] + near
    rest = [k for k in range(chips) if k not in some]

    def second(which):
        return [
            product([second_parts[k] for k in ks], [second_all[k] for k in ks], which)
            for ks in (some, rest)
        ]

    early, late = second(1 - core)
    other = flip((late + (early + first_other)).astype(BF16), 1)
    early, late = second(core)
    grad_query = late + ((early + first_own) + other.astype(F32))

    partial = 0
    for pieces, columns in zip(plane_rows, kv_all):
        size = tokens // len(pieces)
        for i, piece in enumerate(pieces):
            part = columns[i * size : (i + 1) * size]
            partial = partial + jnp.einsum("td,tc->dc", piece, part, preferred_element_type=F32)
    mine, theirs = partial[:, : chip_cols // 2], partial[:, chip_cols // 2 :]
    mine, theirs = jnp.where(core == 0, mine, theirs), jnp.where(core == 0, theirs, mine)
    grad_kv = mine + flip(theirs.astype(BF16), 1).astype(F32)
    device_cols = chip_cols // 4

    return (
        attended.reshape(slots, length, query_cols),
        grad_query,
        grad_kv[:, :device_cols],
        grad_kv[:, device_cols:],
    )


def solution(mesh):
    return jax.shard_map(
        functools.partial(local, mesh.shape["dp"], mesh.shape["mp"]),
        mesh=mesh,
        in_specs=(
            P("dp", None, "mp"),
            P("dp", None),
            P("dp"),
            P("dp"),
            P("dp"),
            P("dp", None, "mp"),
            P(None, "mp"),
            P("mp", None),
            P("mp", None),
            P(),
            P(),
        ),
        out_specs=(P("dp", None, "mp"), P("dp", "mp"), P("mp", "dp"), P("mp", "dp")),
        check_vma=False,
    )
```

```python
import functools
import math

import jax
import jax.numpy as jnp
from jax import lax
from jax.experimental import pallas as pl
from jax.experimental.pallas import tpu as pltpu
from jax.sharding import PartitionSpec as P

HEADS = 32
KV_HEADS = 4
F32 = jnp.float32
BF16 = jnp.bfloat16


def dot(a, b, contract):
    return lax.dot_general(a, b, ((contract[0], contract[1]), ((), ())), preferred_element_type=F32)


def rms_back(values, inverse, gain, grad_out):
    scaled = grad_out * gain
    inner = jnp.mean(values * scaled, axis=-1, keepdims=True)
    return inverse * scaled - values * (inverse * inverse * inverse) * inner


def attend_tile(query, key, value, d_out, query_gain, key_gain, length):
    tokens, dim = key.shape
    heads = query.shape[1] // dim
    scale = 1.0 / math.sqrt(dim)

    def stack(wide):
        return jnp.concatenate([wide[:, h * dim : (h + 1) * dim] for h in range(heads)], axis=0)

    def unstack(tall):
        return jnp.concatenate(
            [tall[h * tokens : (h + 1) * tokens] for h in range(heads)], axis=1
        )

    query = stack(query)
    q_inverse = lax.rsqrt(jnp.mean(query * query, axis=-1, keepdims=True) + 1e-06)
    q_half = (query * q_inverse * query_gain).astype(BF16)
    k_inverse = lax.rsqrt(jnp.mean(key * key, axis=-1, keepdims=True) + 1e-06)
    k_half = (key * k_inverse * key_gain).astype(BF16)
    v_half = value.astype(BF16)
    out_half = stack(d_out).astype(BF16)

    shape = (tokens, tokens)
    row = lax.broadcasted_iota(jnp.int32, shape, 0)
    col = lax.broadcasted_iota(jnp.int32, shape, 1)
    size = jnp.full(shape, length, jnp.int32)
    allowed = (row >= col) & (lax.div(row, size) == lax.div(col, size))
    allowed = jnp.concatenate([allowed] * heads, axis=0)

    scores = dot(q_half, k_half, ((1,), (1,))) * scale
    scores = jnp.where(allowed, scores, -1e30)
    raised = jnp.exp(scores - jnp.max(scores, axis=-1, keepdims=True))
    probs = raised / jnp.sum(raised, axis=-1, keepdims=True)
    p_half = probs.astype(BF16)
    attended = dot(p_half, v_half, ((1,), (0,)))
    d_probs = dot(out_half, v_half, ((1,), (1,)))
    d_value = dot(p_half, out_half, ((0,), (0,)))
    inner = jnp.sum(d_probs * probs, axis=-1, keepdims=True)
    score_half = (probs * (d_probs - inner) * scale).astype(BF16)
    d_qnorm = dot(score_half, k_half, ((1,), (0,)))
    d_knorm = dot(score_half, q_half, ((0,), (0,)))
    d_query = rms_back(query, q_inverse, query_gain, d_qnorm)
    d_key = rms_back(key, k_inverse, key_gain, d_knorm)
    return (
        unstack(attended),
        unstack(d_query),
        d_key,
        d_value,
    )


def attend_kernel(
    length,
    device_cols,
    x_ref,
    wq_ref,
    wkv_ref,
    d_out_ref,
    query_gain_ref,
    key_gain_ref,
    attended_ref,
    dq_ref,
    dkv_ref,
    query_ref,
    kv_ref,
):
    step = pl.program_id(0)
    x = x_ref[0]
    query_part = jnp.dot(x, wq_ref[...], preferred_element_type=F32)
    kv_part = jnp.dot(x, wkv_ref[...], preferred_element_type=F32)

    @pl.when(step == 0)
    def _():
        query_ref[...] = query_part
        kv_ref[...] = kv_part

    @pl.when(step > 0)
    def _():
        query_ref[...] += query_part
        kv_ref[...] += kv_part

    @pl.when(step == pl.num_programs(0) - 1)
    def _():
        tokens = query_ref.shape[0]
        dim = query_gain_ref.shape[1]
        tile = min(tokens, max(1, 128 // length) * length)
        for start in range(0, tokens, tile):
            rows = slice(start, start + tile)
            attended, d_query, d_key, d_value = attend_tile(
                query_ref[rows, :],
                kv_ref[rows, :dim],
                kv_ref[rows, dim:],
                d_out_ref[rows, :],
                query_gain_ref[...],
                key_gain_ref[...],
                length,
            )
            attended_ref[rows, :] = attended
            dq_ref[rows, :] = d_query
            for first in range(0, dim, device_cols):
                columns = slice(first, first + device_cols)
                pair = jnp.concatenate([d_key[:, columns], d_value[:, columns]], axis=1)
                dkv_ref[rows, 2 * first : 2 * first + 2 * device_cols] = pair


def attend(x, w_query, w_kv, d_out, query_gain, key_gain, length, device_cols):
    blocks, tokens, width = x.shape
    cols = w_query.shape[1]
    kv_cols = w_kv.shape[1]
    whole = lambda shape: pl.BlockSpec(shape, lambda b: (0, 0))
    return pl.pallas_call(
        functools.partial(attend_kernel, length, device_cols),
        grid=(blocks,),
        in_specs=[
            pl.BlockSpec((1, tokens, width), lambda b: (b, 0, 0)),
            pl.BlockSpec((width, cols), lambda b: (b, 0)),
            pl.BlockSpec((width, kv_cols), lambda b: (b, 0)),
            whole(d_out.shape),
            whole(query_gain.shape),
            whole(key_gain.shape),
        ],
        out_specs=[whole((tokens, cols)), whole((tokens, cols)), whole((tokens, kv_cols))],
        out_shape=[
            jax.ShapeDtypeStruct((tokens, cols), F32),
            jax.ShapeDtypeStruct((tokens, cols), F32),
            jax.ShapeDtypeStruct((tokens, kv_cols), F32),
        ],
        scratch_shapes=[pltpu.VMEM((tokens, cols), F32), pltpu.VMEM((tokens, kv_cols), F32)],
        compiler_params=pltpu.CompilerParams(vmem_limit_bytes=40 * 1024 * 1024),
        cost_estimate=pl.CostEstimate(
            flops=10 * x.size * (cols + kv_cols),
            bytes_accessed=8 * w_query.size,
            transcendentals=tokens * cols,
        ),
    )(x, w_query, w_kv, d_out, query_gain, key_gain)


def together(*values):
    return lax.optimization_barrier(values)


def pick(array, index):
    return array.at[index].get(mode="promise_in_bounds")


def local(
    n_dp,
    n_mp,
    pool,
    send_table,
    slot_source,
    multiplicity,
    slot_weight,
    cotangent,
    w_query,
    w_key,
    w_value,
    query_gain,
    key_gain,
):
    slots = slot_source.shape[0]
    length = pool.shape[1]
    width = pool.shape[2]
    query_cols = w_query.shape[1]
    key_cols = w_key.shape[1]
    dim = query_gain.shape[0]
    tokens = slots * length
    chips = n_dp // 2
    dp = lax.axis_index("dp")
    mp = lax.axis_index("mp")
    chip, core = dp // 2, dp % 2

    def flip(block, bits):
        return lax.ppermute(block, "dp", [(i, i ^ bits) for i in range(n_dp)])

    def other_chips(blocks):
        return [flip(blocks[k], 2 * k) for k in range(1, chips)]

    def around(blocks):
        return [blocks[0]] + [
            lax.ppermute(blocks[k], "mp", [(i, (i + k) % n_mp) for i in range(n_mp)])
            for k in range(1, n_mp)
        ]

    near = [1 << b for b in range(chips.bit_length() - 1)]

    def from_near(block):
        return [flip(block, 2 * k) for k in near]

    def from_far(block, arrived):
        arrived = dict(zip(near, arrived))
        return [
            block if k == 0 else arrived[k] if k in arrived else flip(block, 2 * k)
            for k in range(chips)
        ]

    outgoing = pick(pool, jnp.maximum(send_table[0], 0))
    outgoing, w_key, w_value = together(outgoing, w_key, w_value)
    arrived = lax.all_to_all(outgoing, "dp", split_axis=0, concat_axis=0, tiled=True)

    share = width // n_dp
    own_key = lax.dynamic_slice_in_dim(w_key, dp * share, share, 0)
    own_value = lax.dynamic_slice_in_dim(w_value, dp * share, share, 0)
    pairs = []
    for head in range(KV_HEADS):
        columns = slice(head * dim, (head + 1) * dim)
        pairs.append(jnp.concatenate([own_key[:, columns], own_value[:, columns]], axis=1))
    pairs = jnp.stack(pairs)
    heads = [(mp + k) % n_mp * KV_HEADS // n_mp for k in range(n_mp)]
    pairs = [lax.dynamic_index_in_dim(pairs, h, 0, False) for h in heads]
    arrived, pairs = lax.optimization_barrier((arrived, pairs))
    shares = jnp.stack(around(pairs))
    rows = pick(arrived, slot_source).reshape(tokens, width)

    x = lax.all_gather(rows, "mp", axis=0)
    shares = jnp.stack([shares] + other_chips([shares] * chips))
    native, shares = together(rows, shares)
    other_shares, *plane_rows = together(flip(shares, 1), *from_near(native))
    plane_rows = jnp.stack(from_far(native, plane_rows)).reshape(chips * tokens, width)

    shares = jnp.stack([shares, other_shares], axis=1).reshape(n_dp * n_mp, share, 2 * dim)
    order = (dp ^ jnp.arange(n_dp))[None, :] * n_mp + ((mp - jnp.arange(n_mp)) % n_mp)[:, None]
    w_kv = pick(shares, order.reshape(-1)).reshape(n_mp * width, 2 * dim)

    x, w_kv, plane_rows = together(x, w_kv, plane_rows)

    chip_width = n_mp * width // chips

    def chip_part(k):
        if chip_width == width:
            return lax.dynamic_index_in_dim(x, chip ^ k, 0, False)
        flat = x.transpose(1, 0, 2).reshape(tokens, -1)
        return lax.dynamic_slice_in_dim(flat, (chip ^ k) * chip_width, chip_width, 1)

    x, *chip_rows = together(x, *[chip_part(k) for k in range(chips)])
    near_rows = [flip(chip_rows[k], 2 * k) for k in near]

    factor = multiplicity.astype(F32) * slot_weight / length
    d_out = (cotangent.astype(F32) * factor[:, None, None]).astype(BF16).astype(F32)
    attended, d_query, d_kv = attend(
        x,
        w_query,
        w_kv,
        d_out.reshape(tokens, query_cols),
        query_gain[None, :],
        key_gain[None, :],
        length,
        key_cols // n_dp,
    )
    attended, d_query, d_kv = [value.astype(BF16) for value in (attended, d_query, d_kv)]
    d_query, d_kv, *near_rows = together(d_query, d_kv, *near_rows)
    chip_rows = [
        chip_rows[0] if k == 0 else near_rows[near.index(k)] if k in near else flip(chip_rows[k], 2 * k)
        for k in range(chips)
    ]
    spread = around([d_kv] * n_mp)
    d_query, spread, chip_rows = lax.optimization_barrier((d_query, spread, chip_rows))
    spread = jnp.stack(spread)

    d_all = [d_query] + other_chips([d_query] * chips)
    half = chip_width // 2
    early = [0] + near
    late = [k for k in range(chips) if k not in early]

    def product(some, which):
        mine = jnp.concatenate([chip_rows[k] for k in some])
        mine = lax.dynamic_slice_in_dim(mine, which * half, half, 1)
        theirs = jnp.concatenate([d_all[k] for k in some])
        return jnp.einsum("td,tc->dc", mine, theirs, preferred_element_type=F32)

    other = flip((product(early, 1 - core) + product(late, 1 - core)).astype(BF16), 1)
    grad_query = product(late, core) + (product(early, core) + other.astype(F32))

    if n_mp > KV_HEADS:
        spread = pick(spread, (mp - jnp.arange(n_mp)) % n_mp)
        spread = spread.reshape(KV_HEADS, n_mp // KV_HEADS, tokens, 2 * dim)
        spread = jnp.sum(spread.astype(F32), axis=1).astype(BF16)
        spread_at = lambda index: index
    else:
        spread_at = lambda index: (mp - index) % n_mp
    chip_cols = 2 * key_cols // chips
    if chip_cols != 2 * dim:
        spread = spread.reshape(KV_HEADS, tokens, chips // KV_HEADS, chip_cols)
        spread = spread.transpose(0, 2, 1, 3).reshape(chips, tokens, chip_cols)
    kv_all = [lax.dynamic_index_in_dim(spread, spread_at(chip ^ k), 0, False) for k in range(chips)]
    kv_all = jnp.stack([kv_all[0]] + other_chips(kv_all)).reshape(chips * tokens, chip_cols)
    partial = jnp.einsum("td,tc->dc", plane_rows, kv_all, preferred_element_type=F32)
    mine, theirs = partial[:, : chip_cols // 2], partial[:, chip_cols // 2 :]
    mine, theirs = jnp.where(core == 0, mine, theirs), jnp.where(core == 0, theirs, mine)
    grad_kv = mine + flip(theirs.astype(BF16), 1).astype(F32)
    device_cols = chip_cols // 4

    return (
        attended.reshape(slots, length, query_cols),
        grad_query,
        grad_kv[:, :device_cols],
        grad_kv[:, device_cols:],
    )


def solution(mesh):
    return jax.shard_map(
        functools.partial(local, mesh.shape["dp"], mesh.shape["mp"]),
        mesh=mesh,
        in_specs=(
            P("dp", None, "mp"),
            P("dp", None),
            P("dp"),
            P("dp"),
            P("dp"),
            P("dp", None, "mp"),
            P(None, "mp"),
            P("mp", None),
            P("mp", None),
            P(),
            P(),
        ),
        out_specs=(P("dp", None, "mp"), P("dp", "mp"), P("mp", "dp"), P("mp", "dp")),
        check_vma=False,
    )
```

```python
import functools
import math

import jax
import jax.numpy as jnp
from jax import lax
from jax.experimental import pallas as pl
from jax.experimental.pallas import tpu as pltpu
from jax.sharding import PartitionSpec as P

HEADS = 32
KV_HEADS = 4
F32 = jnp.float32
BF16 = jnp.bfloat16


def dot(a, b, contract):
    return lax.dot_general(a, b, ((contract[0], contract[1]), ((), ())), preferred_element_type=F32)


def rms_back(values, inverse, gain, grad_out):
    scaled = grad_out * gain
    inner = jnp.mean(values * scaled, axis=-1, keepdims=True)
    return inverse * scaled - values * (inverse * inverse * inverse) * inner


def attend_tile(query, key, value, d_out, query_gain, key_gain, length):
    tokens, dim = key.shape
    heads = query.shape[1] // dim
    scale = 1.0 / math.sqrt(dim)

    def stack(wide):
        return jnp.concatenate([wide[:, h * dim : (h + 1) * dim] for h in range(heads)], axis=0)

    def unstack(tall):
        return jnp.concatenate(
            [tall[h * tokens : (h + 1) * tokens] for h in range(heads)], axis=1
        )

    query = stack(query)
    q_inverse = lax.rsqrt(jnp.mean(query * query, axis=-1, keepdims=True) + 1e-06)
    q_half = (query * q_inverse * query_gain).astype(BF16)
    k_inverse = lax.rsqrt(jnp.mean(key * key, axis=-1, keepdims=True) + 1e-06)
    k_half = (key * k_inverse * key_gain).astype(BF16)
    v_half = value.astype(BF16)
    out_half = stack(d_out).astype(BF16)

    shape = (tokens, tokens)
    row = lax.broadcasted_iota(jnp.int32, shape, 0)
    col = lax.broadcasted_iota(jnp.int32, shape, 1)
    size = jnp.full(shape, length, jnp.int32)
    allowed = (row >= col) & (lax.div(row, size) == lax.div(col, size))
    allowed = jnp.concatenate([allowed] * heads, axis=0)

    scores = dot(q_half, k_half, ((1,), (1,))) * scale
    scores = jnp.where(allowed, scores, -1e30)
    raised = jnp.exp(scores - jnp.max(scores, axis=-1, keepdims=True))
    probs = raised / jnp.sum(raised, axis=-1, keepdims=True)
    p_half = probs.astype(BF16)
    attended = dot(p_half, v_half, ((1,), (0,)))
    d_probs = dot(out_half, v_half, ((1,), (1,)))
    d_value = dot(p_half, out_half, ((0,), (0,)))
    inner = jnp.sum(d_probs * probs, axis=-1, keepdims=True)
    score_half = (probs * (d_probs - inner) * scale).astype(BF16)
    d_qnorm = dot(score_half, k_half, ((1,), (0,)))
    d_knorm = dot(score_half, q_half, ((0,), (0,)))
    d_query = rms_back(query, q_inverse, query_gain, d_qnorm)
    d_key = rms_back(key, k_inverse, key_gain, d_knorm)
    return (
        unstack(attended),
        unstack(d_query),
        d_key,
        d_value,
    )


def attend_kernel(
    length,
    device_cols,
    x_ref,
    wq_ref,
    wkv_ref,
    d_out_ref,
    query_gain_ref,
    key_gain_ref,
    attended_ref,
    dq_ref,
    dkv_ref,
    query_ref,
    kv_ref,
):
    step = pl.program_id(0)
    x = x_ref[0]
    query_part = jnp.dot(x, wq_ref[...], preferred_element_type=F32)
    kv_part = jnp.dot(x, wkv_ref[...], preferred_element_type=F32)

    @pl.when(step == 0)
    def _():
        query_ref[...] = query_part
        kv_ref[...] = kv_part

    @pl.when(step > 0)
    def _():
        query_ref[...] += query_part
        kv_ref[...] += kv_part

    @pl.when(step == pl.num_programs(0) - 1)
    def _():
        tokens = query_ref.shape[0]
        dim = query_gain_ref.shape[1]
        tile = min(tokens, max(1, 128 // length) * length)
        for start in range(0, tokens, tile):
            rows = slice(start, start + tile)
            attended, d_query, d_key, d_value = attend_tile(
                query_ref[rows, :],
                kv_ref[rows, :dim],
                kv_ref[rows, dim:],
                d_out_ref[rows, :],
                query_gain_ref[...],
                key_gain_ref[...],
                length,
            )
            attended_ref[rows, :] = attended
            dq_ref[rows, :] = d_query
            for first in range(0, dim, device_cols):
                columns = slice(first, first + device_cols)
                pair = jnp.concatenate([d_key[:, columns], d_value[:, columns]], axis=1)
                dkv_ref[rows, 2 * first : 2 * first + 2 * device_cols] = pair


def attend(x, w_query, w_kv, d_out, query_gain, key_gain, length, device_cols):
    blocks, tokens, width = x.shape
    cols = w_query.shape[1]
    kv_cols = w_kv.shape[1]
    whole = lambda shape: pl.BlockSpec(shape, lambda b: (0, 0))
    return pl.pallas_call(
        functools.partial(attend_kernel, length, device_cols),
        grid=(blocks,),
        in_specs=[
            pl.BlockSpec((1, tokens, width), lambda b: (b, 0, 0)),
            pl.BlockSpec((width, cols), lambda b: (b, 0)),
            pl.BlockSpec((width, kv_cols), lambda b: (b, 0)),
            whole(d_out.shape),
            whole(query_gain.shape),
            whole(key_gain.shape),
        ],
        out_specs=[whole((tokens, cols)), whole((tokens, cols)), whole((tokens, kv_cols))],
        out_shape=[
            jax.ShapeDtypeStruct((tokens, cols), F32),
            jax.ShapeDtypeStruct((tokens, cols), F32),
            jax.ShapeDtypeStruct((tokens, kv_cols), F32),
        ],
        scratch_shapes=[pltpu.VMEM((tokens, cols), F32), pltpu.VMEM((tokens, kv_cols), F32)],
        compiler_params=pltpu.CompilerParams(vmem_limit_bytes=40 * 1024 * 1024),
        cost_estimate=pl.CostEstimate(
            flops=20 * x.size * (cols + kv_cols),
            bytes_accessed=8 * w_query.size,
            transcendentals=tokens * cols,
        ),
    )(x, w_query, w_kv, d_out, query_gain, key_gain)


def together(*values):
    return lax.optimization_barrier(values)


def pick(array, index):
    return array.at[index].get(mode="promise_in_bounds")


def local(
    n_dp,
    n_mp,
    pool,
    send_table,
    slot_source,
    multiplicity,
    slot_weight,
    cotangent,
    w_query,
    w_key,
    w_value,
    query_gain,
    key_gain,
):
    slots = slot_source.shape[0]
    length = pool.shape[1]
    width = pool.shape[2]
    query_cols = w_query.shape[1]
    key_cols = w_key.shape[1]
    dim = query_gain.shape[0]
    tokens = slots * length
    chips = n_dp // 2
    dp = lax.axis_index("dp")
    mp = lax.axis_index("mp")
    chip, core = dp // 2, dp % 2

    def flip(block, bits):
        return lax.ppermute(block, "dp", [(i, i ^ bits) for i in range(n_dp)])

    def other_chips(blocks):
        return [flip(blocks[k], 2 * k) for k in range(1, chips)]

    def around(blocks):
        return [blocks[0]] + [
            lax.ppermute(blocks[k], "mp", [(i, (i + k) % n_mp) for i in range(n_mp)])
            for k in range(1, n_mp)
        ]

    near = [1 << b for b in range(chips.bit_length() - 1)]

    def from_near(block):
        return [flip(block, 2 * k) for k in near]

    def from_far(block, arrived):
        arrived = dict(zip(near, arrived))
        middle = block.shape[0] // 2
        pieces = [[block]]
        for k in range(1, chips):
            bits = [n for n in near if k & n]
            if len(bits) == 1:
                pieces.append([arrived[k]])
            elif len(bits) == 2:
                first = flip(arrived[bits[0]][:middle], 2 * bits[1])
                second = flip(arrived[bits[1]][middle:], 2 * bits[0])
                pieces.append([first, second])
            else:
                pieces.append([flip(block, 2 * k)])
        return pieces

    outgoing = pick(pool, jnp.maximum(send_table[0], 0))
    outgoing, w_key, w_value = together(outgoing, w_key, w_value)
    arrived = lax.all_to_all(outgoing, "dp", split_axis=0, concat_axis=0, tiled=True)

    share = width // n_dp
    own_key = lax.dynamic_slice_in_dim(w_key, dp * share, share, 0)
    own_value = lax.dynamic_slice_in_dim(w_value, dp * share, share, 0)
    pairs = []
    for head in range(KV_HEADS):
        columns = slice(head * dim, (head + 1) * dim)
        pairs.append(jnp.concatenate([own_key[:, columns], own_value[:, columns]], axis=1))
    pairs = jnp.stack(pairs)
    heads = [(mp + k) % n_mp * KV_HEADS // n_mp for k in range(n_mp)]
    shares = around([lax.dynamic_index_in_dim(pairs, h, 0, False) for h in heads])
    shares = jnp.stack(shares)
    rows = pick(arrived, slot_source).reshape(tokens, width)

    middle = tokens // 2
    first_rows, second_rows = rows[:middle], rows[middle:]
    x_first = lax.all_gather(first_rows, "mp", axis=0)
    shares = jnp.stack([shares] + other_chips([shares] * chips))
    native, second_rows, shares = together(rows, second_rows, shares)
    x_second = lax.all_gather(second_rows, "mp", axis=0)
    other_shares = flip(shares, 1)
    plane_rows = together(*from_near(native))
    plane_rows = from_far(native, plane_rows)

    shares = jnp.stack([shares, other_shares], axis=1).reshape(n_dp * n_mp, share, 2 * dim)
    order = (dp ^ jnp.arange(n_dp))[None, :] * n_mp + ((mp - jnp.arange(n_mp)) % n_mp)[:, None]
    w_kv = pick(shares, order.reshape(-1)).reshape(n_mp * width, 2 * dim)

    factor = multiplicity.astype(F32) * slot_weight / length
    d_out = (cotangent.astype(F32) * factor[:, None, None]).astype(BF16).astype(F32)
    d_out = d_out.reshape(tokens, query_cols)
    chip_width = n_mp * width // chips

    def chip_part(x, k):
        if chip_width == width:
            return lax.dynamic_index_in_dim(x, chip ^ k, 0, False)
        flat = x.transpose(1, 0, 2).reshape(x.shape[1], -1)
        return lax.dynamic_slice_in_dim(flat, (chip ^ k) * chip_width, chip_width, 1)

    def half_step(x, d_out, beside):
        x, *parts = together(x, *[chip_part(x, k) for k in range(chips)])
        near_parts = [flip(parts[k], 2 * k) for k in near]
        attended, d_query, d_kv = attend(
            x, w_query, w_kv, d_out, query_gain[None, :], key_gain[None, :], length, key_cols // n_dp
        )
        d_query, d_kv, near_parts, beside = lax.optimization_barrier(
            (d_query.astype(BF16), d_kv.astype(BF16), near_parts, beside)
        )
        near_parts = dict(zip(near, near_parts))
        for k in range(1, chips):
            parts[k] = near_parts[k] if k in near_parts else flip(parts[k], 2 * k)
        d_query, *parts = together(d_query, *parts)
        return attended.astype(BF16), d_query, d_kv, parts, beside

    (x_first, *native_near) = together(x_first, *[plane_rows[k][0] for k in near])
    for k, block in zip(near, native_near):
        plane_rows[k] = [block]
    attended, d_query, d_kv, first_parts, plane_rows = half_step(
        x_first, d_out[:middle], plane_rows
    )
    plane_rows = jnp.concatenate([piece for pieces in plane_rows for piece in pieces])
    x_second, first_parts, plane_rows, d_query, d_kv = lax.optimization_barrier(
        (x_second, first_parts, plane_rows, d_query, d_kv)
    )
    attended_second, d_query_second, d_kv_second, second_parts, beside = half_step(
        x_second, d_out[middle:], (attended, first_parts, d_query, d_kv)
    )
    attended, first_parts, d_query, d_kv = beside
    attended = jnp.concatenate([attended, attended_second])
    d_query = jnp.concatenate([d_query, d_query_second])
    d_kv = jnp.concatenate([d_kv, d_kv_second])

    d_all = [d_query] + other_chips([d_query] * chips)
    spread = jnp.stack(around([d_kv] * n_mp))
    half = chip_width // 2
    early = [0] + near
    late = [k for k in range(chips) if k not in early]

    def product(some, which):
        mine = jnp.concatenate([part[k] for k in some for part in (first_parts, second_parts)])
        mine = lax.dynamic_slice_in_dim(mine, which * half, half, 1)
        theirs = jnp.concatenate([d_all[k] for k in some])
        return jnp.einsum("td,tc->dc", mine, theirs, preferred_element_type=F32)

    other = flip((product(early, 1 - core) + product(late, 1 - core)).astype(BF16), 1)
    grad_query = product(late, core) + (product(early, core) + other.astype(F32))

    if n_mp > KV_HEADS:
        spread = pick(spread, (mp - jnp.arange(n_mp)) % n_mp)
        spread = spread.reshape(KV_HEADS, n_mp // KV_HEADS, tokens, 2 * dim)
        spread = jnp.sum(spread.astype(F32), axis=1).astype(BF16)
        spread_at = lambda index: index
    else:
        spread_at = lambda index: (mp - index) % n_mp
    chip_cols = 2 * key_cols // chips
    if chip_cols != 2 * dim:
        spread = spread.reshape(KV_HEADS, tokens, chips // KV_HEADS, chip_cols)
        spread = spread.transpose(0, 2, 1, 3).reshape(chips, tokens, chip_cols)
    kv_all = [lax.dynamic_index_in_dim(spread, spread_at(chip ^ k), 0, False) for k in range(chips)]
    kv_all = jnp.concatenate([kv_all[0]] + other_chips(kv_all))
    partial = jnp.einsum("td,tc->dc", plane_rows, kv_all, preferred_element_type=F32)
    mine, theirs = partial[:, : chip_cols // 2], partial[:, chip_cols // 2 :]
    mine, theirs = jnp.where(core == 0, mine, theirs), jnp.where(core == 0, theirs, mine)
    grad_kv = mine + flip(theirs.astype(BF16), 1).astype(F32)
    device_cols = chip_cols // 4

    return (
        attended.reshape(slots, length, query_cols),
        grad_query,
        grad_kv[:, :device_cols],
        grad_kv[:, device_cols:],
    )


def solution(mesh):
    return jax.shard_map(
        functools.partial(local, mesh.shape["dp"], mesh.shape["mp"]),
        mesh=mesh,
        in_specs=(
            P("dp", None, "mp"),
            P("dp", None),
            P("dp"),
            P("dp"),
            P("dp"),
            P("dp", None, "mp"),
            P(None, "mp"),
            P("mp", None),
            P("mp", None),
            P(),
            P(),
        ),
        out_specs=(P("dp", None, "mp"), P("dp", "mp"), P("mp", "dp"), P("mp", "dp")),
        check_vma=False,
    )
```

```python
import functools
import math

import jax
import jax.numpy as jnp
from jax import lax
from jax.experimental import pallas as pl
from jax.experimental.pallas import tpu as pltpu
from jax.sharding import PartitionSpec as P

HEADS = 32
KV_HEADS = 4
F32 = jnp.float32
BF16 = jnp.bfloat16


def dot(a, b, contract):
    return lax.dot_general(a, b, ((contract[0], contract[1]), ((), ())), preferred_element_type=F32)


def rms_back(values, inverse, gain, grad_out):
    scaled = grad_out * gain
    inner = jnp.mean(values * scaled, axis=-1, keepdims=True)
    return inverse * scaled - values * (inverse * inverse * inverse) * inner


def attend_tile(query, key, value, d_out, query_gain, key_gain, length):
    tokens, dim = key.shape
    heads = query.shape[1] // dim
    scale = 1.0 / math.sqrt(dim)

    def stack(wide):
        return jnp.concatenate([wide[:, h * dim : (h + 1) * dim] for h in range(heads)], axis=0)

    def unstack(tall):
        return jnp.concatenate(
            [tall[h * tokens : (h + 1) * tokens] for h in range(heads)], axis=1
        )

    query = stack(query)
    q_inverse = lax.rsqrt(jnp.mean(query * query, axis=-1, keepdims=True) + 1e-06)
    q_half = (query * q_inverse * query_gain).astype(BF16)
    k_inverse = lax.rsqrt(jnp.mean(key * key, axis=-1, keepdims=True) + 1e-06)
    k_half = (key * k_inverse * key_gain).astype(BF16)
    v_half = value.astype(BF16)
    out_half = stack(d_out).astype(BF16)

    shape = (tokens, tokens)
    row = lax.broadcasted_iota(jnp.int32, shape, 0)
    col = lax.broadcasted_iota(jnp.int32, shape, 1)
    size = jnp.full(shape, length, jnp.int32)
    allowed = (row >= col) & (lax.div(row, size) == lax.div(col, size))
    allowed = jnp.concatenate([allowed] * heads, axis=0)

    scores = dot(q_half, k_half, ((1,), (1,))) * scale
    scores = jnp.where(allowed, scores, -1e30)
    raised = jnp.exp(scores - jnp.max(scores, axis=-1, keepdims=True))
    probs = raised / jnp.sum(raised, axis=-1, keepdims=True)
    p_half = probs.astype(BF16)
    attended = dot(p_half, v_half, ((1,), (0,)))
    d_probs = dot(out_half, v_half, ((1,), (1,)))
    d_value = dot(p_half, out_half, ((0,), (0,)))
    inner = jnp.sum(d_probs * probs, axis=-1, keepdims=True)
    score_half = (probs * (d_probs - inner) * scale).astype(BF16)
    d_qnorm = dot(score_half, k_half, ((1,), (0,)))
    d_knorm = dot(score_half, q_half, ((0,), (0,)))
    d_query = rms_back(query, q_inverse, query_gain, d_qnorm)
    d_key = rms_back(key, k_inverse, key_gain, d_knorm)
    return (
        unstack(attended),
        unstack(d_query),
        d_key,
        d_value,
    )


def attend_kernel(
    length,
    device_cols,
    x_ref,
    wq_ref,
    wkv_ref,
    d_out_ref,
    query_gain_ref,
    key_gain_ref,
    attended_ref,
    dq_ref,
    dkv_ref,
    query_ref,
    kv_ref,
):
    step = pl.program_id(0)
    x = x_ref[...]
    query_part = jnp.dot(x, wq_ref[...], preferred_element_type=F32)
    kv_part = jnp.dot(x, wkv_ref[...], preferred_element_type=F32)

    @pl.when(step == 0)
    def _():
        query_ref[...] = query_part
        kv_ref[...] = kv_part

    @pl.when(step > 0)
    def _():
        query_ref[...] += query_part
        kv_ref[...] += kv_part

    @pl.when(step == pl.num_programs(0) - 1)
    def _():
        tokens = query_ref.shape[0]
        dim = query_gain_ref.shape[1]
        tile = min(tokens, max(1, 128 // length) * length)
        for start in range(0, tokens, tile):
            rows = slice(start, start + tile)
            attended, d_query, d_key, d_value = attend_tile(
                query_ref[rows, :],
                kv_ref[rows, :dim],
                kv_ref[rows, dim:],
                d_out_ref[rows, :],
                query_gain_ref[...],
                key_gain_ref[...],
                length,
            )
            attended_ref[rows, :] = attended
            dq_ref[rows, :] = d_query
            for first in range(0, dim, device_cols):
                columns = slice(first, first + device_cols)
                pair = jnp.concatenate([d_key[:, columns], d_value[:, columns]], axis=1)
                dkv_ref[rows, 2 * first : 2 * first + 2 * device_cols] = pair


def attend(x, w_query, w_kv, d_out, query_gain, key_gain, length, device_cols):
    tokens, depth = x.shape
    cols = w_query.shape[1]
    kv_cols = w_kv.shape[1]
    block = depth // 4
    whole = lambda shape: pl.BlockSpec(shape, lambda b: (0, 0))
    return pl.pallas_call(
        functools.partial(attend_kernel, length, device_cols),
        grid=(depth // block,),
        in_specs=[
            pl.BlockSpec((tokens, block), lambda b: (0, b)),
            pl.BlockSpec((block, cols), lambda b: (b, 0)),
            pl.BlockSpec((block, kv_cols), lambda b: (b, 0)),
            whole(d_out.shape),
            whole(query_gain.shape),
            whole(key_gain.shape),
        ],
        out_specs=[whole((tokens, cols)), whole((tokens, cols)), whole((tokens, kv_cols))],
        out_shape=[
            jax.ShapeDtypeStruct((tokens, cols), F32),
            jax.ShapeDtypeStruct((tokens, cols), F32),
            jax.ShapeDtypeStruct((tokens, kv_cols), F32),
        ],
        scratch_shapes=[pltpu.VMEM((tokens, cols), F32), pltpu.VMEM((tokens, kv_cols), F32)],
        compiler_params=pltpu.CompilerParams(vmem_limit_bytes=40 * 1024 * 1024),
        cost_estimate=pl.CostEstimate(
            flops=10 * tokens * depth * (cols + kv_cols),
            bytes_accessed=8 * w_query.size,
            transcendentals=tokens * cols,
        ),
    )(x, w_query, w_kv, d_out, query_gain, key_gain)


def together(*values):
    return lax.optimization_barrier(values)


def pick(array, index):
    return array.at[index].get(mode="promise_in_bounds")


def local(
    n_dp,
    n_mp,
    pool,
    send_table,
    slot_source,
    multiplicity,
    slot_weight,
    cotangent,
    w_query,
    w_key,
    w_value,
    query_gain,
    key_gain,
):
    slots = slot_source.shape[0]
    length = pool.shape[1]
    width = pool.shape[2]
    query_cols = w_query.shape[1]
    key_cols = w_key.shape[1]
    dim = query_gain.shape[0]
    tokens = slots * length
    chips = n_dp // 2
    dp = lax.axis_index("dp")
    mp = lax.axis_index("mp")
    chip, core = dp // 2, dp % 2

    def flip(block, bits):
        return lax.ppermute(block, "dp", [(i, i ^ bits) for i in range(n_dp)])

    def other_chips(blocks):
        return [flip(blocks[k], 2 * k) for k in range(1, chips)]

    def around(blocks):
        return [blocks[0]] + [
            lax.ppermute(blocks[k], "mp", [(i, (i + k) % n_mp) for i in range(n_mp)])
            for k in range(1, n_mp)
        ]

    near = [1 << b for b in range(chips.bit_length() - 1)]

    def from_near(block):
        return [flip(block, 2 * k) for k in near]

    def from_far(block, arrived):
        arrived = dict(zip(near, arrived))
        middle = block.shape[0] // 2
        blocks = [block]
        for k in range(1, chips):
            bits = [n for n in near if k & n]
            if len(bits) == 1:
                blocks.append(arrived[k])
            elif len(bits) == 2:
                first = flip(arrived[bits[0]][:middle], 2 * bits[1])
                second = flip(arrived[bits[1]][middle:], 2 * bits[0])
                blocks.append(jnp.concatenate([first, second]))
            else:
                blocks.append(flip(block, 2 * k))
        return blocks

    outgoing = pick(pool, jnp.maximum(send_table[0], 0))
    outgoing, w_key, w_value = together(outgoing, w_key, w_value)
    arrived = lax.all_to_all(outgoing, "dp", split_axis=0, concat_axis=0, tiled=True)

    share = width // n_dp
    own_key = lax.dynamic_slice_in_dim(w_key, dp * share, share, 0)
    own_value = lax.dynamic_slice_in_dim(w_value, dp * share, share, 0)
    pairs = []
    for head in range(KV_HEADS):
        columns = slice(head * dim, (head + 1) * dim)
        pairs.append(jnp.concatenate([own_key[:, columns], own_value[:, columns]], axis=1))
    pairs = jnp.stack(pairs)
    heads = [(mp + k) % n_mp * KV_HEADS // n_mp for k in range(n_mp)]
    shares = around([lax.dynamic_index_in_dim(pairs, h, 0, False) for h in heads])
    arrived, *shares = together(arrived, *shares)
    shares = jnp.stack(shares)
    if n_dp == slots:
        slot_of = jnp.argmax(slot_source[None, :] == jnp.arange(n_dp)[:, None], axis=1)
        place_of = slot_source
    else:
        arrived = pick(arrived, slot_source)
        slot_of = place_of = jnp.arange(slots)
    rows = arrived.reshape(tokens, width)

    x = lax.all_gather(rows, "mp", axis=1, tiled=True)
    shares = jnp.stack([shares] + other_chips([shares] * chips))
    native, shares = together(rows, shares)
    other_shares, *plane_rows = together(flip(shares, 1), *from_near(native))
    plane_rows = jnp.stack(from_far(native, plane_rows)).reshape(chips * tokens, width)

    shares = jnp.stack([shares, other_shares], axis=1).reshape(n_dp * n_mp, share, 2 * dim)
    order = (dp ^ jnp.arange(n_dp))[None, :] * n_mp + ((mp - jnp.arange(n_mp)) % n_mp)[:, None]
    w_kv = pick(shares, order.reshape(-1)).reshape(n_mp * width, 2 * dim)

    x, w_kv, plane_rows = together(x, w_kv, plane_rows)

    chip_width = n_mp * width // chips
    chip_rows = [
        lax.dynamic_slice_in_dim(x, (chip ^ k) * chip_width, chip_width, 1) for k in range(chips)
    ]
    x, *chip_rows = together(x, *chip_rows)
    chip_rows = [chip_rows[0]] + other_chips(chip_rows)

    factor = multiplicity.astype(F32) * slot_weight / length
    d_out = pick(cotangent, slot_of).astype(F32) * pick(factor, slot_of)[:, None, None]
    d_out = d_out.astype(BF16).astype(F32)
    attended, d_query, d_kv = attend(
        x,
        w_query,
        w_kv,
        d_out.reshape(tokens, query_cols),
        query_gain[None, :],
        key_gain[None, :],
        length,
        key_cols // n_dp,
    )
    attended, d_query, d_kv = [value.astype(BF16) for value in (attended, d_query, d_kv)]
    spread = around([d_kv] * n_mp)
    d_query, spread, chip_rows = lax.optimization_barrier((d_query, spread, chip_rows))
    spread = jnp.stack(spread)

    d_all = [d_query] + other_chips([d_query] * chips)
    half = chip_width // 2
    early = [0] + near
    late = [k for k in range(chips) if k not in early]

    def product(some, which):
        mine = jnp.concatenate([chip_rows[k] for k in some])
        mine = lax.dynamic_slice_in_dim(mine, which * half, half, 1)
        theirs = jnp.concatenate([d_all[k] for k in some])
        return jnp.einsum("td,tc->dc", mine, theirs, preferred_element_type=F32)

    other = flip((product(early, 1 - core) + product(late, 1 - core)).astype(BF16), 1)
    grad_query = product(late, core) + (product(early, core) + other.astype(F32))

    if n_mp > KV_HEADS:
        spread = pick(spread, (mp - jnp.arange(n_mp)) % n_mp)
        spread = spread.reshape(KV_HEADS, n_mp // KV_HEADS, tokens, 2 * dim)
        spread = jnp.sum(spread.astype(F32), axis=1).astype(BF16)
        spread_at = lambda index: index
    else:
        spread_at = lambda index: (mp - index) % n_mp
    chip_cols = 2 * key_cols // chips
    if chip_cols != 2 * dim:
        spread = spread.reshape(KV_HEADS, tokens, chips // KV_HEADS, chip_cols)
        spread = spread.transpose(0, 2, 1, 3).reshape(chips, tokens, chip_cols)
    kv_all = [lax.dynamic_index_in_dim(spread, spread_at(chip ^ k), 0, False) for k in range(chips)]
    kv_all = jnp.stack([kv_all[0]] + other_chips(kv_all)).reshape(chips * tokens, chip_cols)
    partial = jnp.einsum("td,tc->dc", plane_rows, kv_all, preferred_element_type=F32)
    mine, theirs = partial[:, : chip_cols // 2], partial[:, chip_cols // 2 :]
    mine, theirs = jnp.where(core == 0, mine, theirs), jnp.where(core == 0, theirs, mine)
    grad_kv = mine + flip(theirs.astype(BF16), 1).astype(F32)
    device_cols = chip_cols // 4

    return (
        pick(attended.reshape(slots, length, query_cols), place_of),
        grad_query,
        grad_kv[:, :device_cols],
        grad_kv[:, device_cols:],
    )


def solution(mesh):
    return jax.shard_map(
        functools.partial(local, mesh.shape["dp"], mesh.shape["mp"]),
        mesh=mesh,
        in_specs=(
            P("dp", None, "mp"),
            P("dp", None),
            P("dp"),
            P("dp"),
            P("dp"),
            P("dp", None, "mp"),
            P(None, "mp"),
            P("mp", None),
            P("mp", None),
            P(),
            P(),
        ),
        out_specs=(P("dp", None, "mp"), P("dp", "mp"), P("mp", "dp"), P("mp", "dp")),
        check_vma=False,
    )
```

```python
import functools
import math

import jax
import jax.numpy as jnp
from jax import lax
from jax.experimental import pallas as pl
from jax.experimental.pallas import tpu as pltpu
from jax.sharding import PartitionSpec as P

HEADS = 32
KV_HEADS = 4
F32 = jnp.float32
BF16 = jnp.bfloat16


def dot(a, b, contract):
    return lax.dot_general(a, b, ((contract[0], contract[1]), ((), ())), preferred_element_type=F32)


def rms_back(values, inverse, gain, grad_out):
    scaled = grad_out * gain
    inner = jnp.mean(values * scaled, axis=-1, keepdims=True)
    return inverse * scaled - values * (inverse * inverse * inverse) * inner


def attend_tile(query, key, value, d_out, query_gain, key_gain, length):
    tokens, dim = key.shape
    heads = query.shape[1] // dim
    scale = 1.0 / math.sqrt(dim)

    def stack(wide):
        return jnp.concatenate([wide[:, h * dim : (h + 1) * dim] for h in range(heads)], axis=0)

    def unstack(tall):
        return jnp.concatenate(
            [tall[h * tokens : (h + 1) * tokens] for h in range(heads)], axis=1
        )

    query = stack(query)
    q_inverse = lax.rsqrt(jnp.mean(query * query, axis=-1, keepdims=True) + 1e-06)
    q_half = (query * q_inverse * query_gain).astype(BF16)
    k_inverse = lax.rsqrt(jnp.mean(key * key, axis=-1, keepdims=True) + 1e-06)
    k_half = (key * k_inverse * key_gain).astype(BF16)
    v_half = value.astype(BF16)
    out_half = stack(d_out).astype(BF16)

    shape = (tokens, tokens)
    row = lax.broadcasted_iota(jnp.int32, shape, 0)
    col = lax.broadcasted_iota(jnp.int32, shape, 1)
    size = jnp.full(shape, length, jnp.int32)
    allowed = (row >= col) & (lax.div(row, size) == lax.div(col, size))
    allowed = jnp.concatenate([allowed] * heads, axis=0)

    scores = dot(q_half, k_half, ((1,), (1,))) * scale
    scores = jnp.where(allowed, scores, -1e30)
    raised = jnp.exp(scores - jnp.max(scores, axis=-1, keepdims=True))
    probs = raised / jnp.sum(raised, axis=-1, keepdims=True)
    p_half = probs.astype(BF16)
    attended = dot(p_half, v_half, ((1,), (0,)))
    d_probs = dot(out_half, v_half, ((1,), (1,)))
    d_value = dot(p_half, out_half, ((0,), (0,)))
    inner = jnp.sum(d_probs * probs, axis=-1, keepdims=True)
    score_half = (probs * (d_probs - inner) * scale).astype(BF16)
    d_qnorm = dot(score_half, k_half, ((1,), (0,)))
    d_knorm = dot(score_half, q_half, ((0,), (0,)))
    d_query = rms_back(query, q_inverse, query_gain, d_qnorm)
    d_key = rms_back(key, k_inverse, key_gain, d_knorm)
    return (
        unstack(attended),
        unstack(d_query),
        d_key,
        d_value,
    )


def attend_kernel(
    length,
    device_cols,
    x_ref,
    wq_ref,
    wkv_ref,
    d_out_ref,
    query_gain_ref,
    key_gain_ref,
    attended_ref,
    dq_ref,
    dkv_ref,
    query_ref,
    kv_ref,
):
    step = pl.program_id(0)
    x = x_ref[...]
    query_part = jnp.dot(x, wq_ref[...], preferred_element_type=F32)
    kv_part = jnp.dot(x, wkv_ref[...], preferred_element_type=F32)

    @pl.when(step == 0)
    def _():
        query_ref[...] = query_part
        kv_ref[...] = kv_part

    @pl.when(step > 0)
    def _():
        query_ref[...] += query_part
        kv_ref[...] += kv_part

    @pl.when(step == pl.num_programs(0) - 1)
    def _():
        tokens = query_ref.shape[0]
        dim = query_gain_ref.shape[1]
        tile = min(tokens, max(1, 128 // length) * length)
        for start in range(0, tokens, tile):
            rows = slice(start, start + tile)
            attended, d_query, d_key, d_value = attend_tile(
                query_ref[rows, :],
                kv_ref[rows, :dim],
                kv_ref[rows, dim:],
                d_out_ref[rows, :],
                query_gain_ref[...],
                key_gain_ref[...],
                length,
            )
            attended_ref[rows, :] = attended
            dq_ref[rows, :] = d_query
            for first in range(0, dim, device_cols):
                columns = slice(first, first + device_cols)
                pair = jnp.concatenate([d_key[:, columns], d_value[:, columns]], axis=1)
                dkv_ref[rows, 2 * first : 2 * first + 2 * device_cols] = pair


def attend(x, w_query, w_kv, d_out, query_gain, key_gain, length, device_cols):
    tokens, depth = x.shape
    cols = w_query.shape[1]
    kv_cols = w_kv.shape[1]
    block = depth // 4
    whole = lambda shape: pl.BlockSpec(shape, lambda b: (0, 0))
    return pl.pallas_call(
        functools.partial(attend_kernel, length, device_cols),
        grid=(depth // block,),
        in_specs=[
            pl.BlockSpec((tokens, block), lambda b: (0, b)),
            pl.BlockSpec((block, cols), lambda b: (b, 0)),
            pl.BlockSpec((block, kv_cols), lambda b: (b, 0)),
            whole(d_out.shape),
            whole(query_gain.shape),
            whole(key_gain.shape),
        ],
        out_specs=[whole((tokens, cols)), whole((tokens, cols)), whole((tokens, kv_cols))],
        out_shape=[
            jax.ShapeDtypeStruct((tokens, cols), F32),
            jax.ShapeDtypeStruct((tokens, cols), F32),
            jax.ShapeDtypeStruct((tokens, kv_cols), F32),
        ],
        scratch_shapes=[pltpu.VMEM((tokens, cols), F32), pltpu.VMEM((tokens, kv_cols), F32)],
        compiler_params=pltpu.CompilerParams(vmem_limit_bytes=40 * 1024 * 1024),
        cost_estimate=pl.CostEstimate(
            flops=10 * tokens * depth * (cols + kv_cols),
            bytes_accessed=8 * w_query.size,
            transcendentals=tokens * cols,
        ),
    )(x, w_query, w_kv, d_out, query_gain, key_gain)


def together(*values):
    return lax.optimization_barrier(values)


def pick(array, index):
    return array.at[index].get(mode="promise_in_bounds")


def local(
    n_dp,
    n_mp,
    pool,
    send_table,
    slot_source,
    multiplicity,
    slot_weight,
    cotangent,
    w_query,
    w_key,
    w_value,
    query_gain,
    key_gain,
):
    slots = slot_source.shape[0]
    length = pool.shape[1]
    width = pool.shape[2]
    query_cols = w_query.shape[1]
    key_cols = w_key.shape[1]
    dim = query_gain.shape[0]
    tokens = slots * length
    chips = n_dp // 2
    dp = lax.axis_index("dp")
    mp = lax.axis_index("mp")
    chip, core = dp // 2, dp % 2

    def flip(block, bits):
        return lax.ppermute(block, "dp", [(i, i ^ bits) for i in range(n_dp)])

    def other_chips(blocks):
        return [flip(blocks[k], 2 * k) for k in range(1, chips)]

    def around(blocks):
        return [blocks[0]] + [
            lax.ppermute(blocks[k], "mp", [(i, (i + k) % n_mp) for i in range(n_mp)])
            for k in range(1, n_mp)
        ]

    near = [1 << b for b in range(chips.bit_length() - 1)]

    def from_near(block):
        return [flip(block, 2 * k) for k in near]

    def from_far(block, arrived):
        arrived = dict(zip(near, arrived))
        middle = block.shape[0] // 2
        blocks = [block]
        for k in range(1, chips):
            bits = [n for n in near if k & n]
            if len(bits) == 1:
                blocks.append(arrived[k])
            elif len(bits) == 2:
                first = flip(arrived[bits[0]][:middle], 2 * bits[1])
                second = flip(arrived[bits[1]][middle:], 2 * bits[0])
                blocks.append(jnp.concatenate([first, second]))
            else:
                blocks.append(flip(block, 2 * k))
        return blocks

    outgoing = pick(pool, jnp.maximum(send_table[0], 0))
    outgoing, w_key, w_value = together(outgoing, w_key, w_value)
    arrived = lax.all_to_all(outgoing, "dp", split_axis=0, concat_axis=0, tiled=True)

    share = width // n_dp
    own_key = lax.dynamic_slice_in_dim(w_key, dp * share, share, 0)
    own_value = lax.dynamic_slice_in_dim(w_value, dp * share, share, 0)
    pairs = []
    for head in range(KV_HEADS):
        columns = slice(head * dim, (head + 1) * dim)
        pairs.append(jnp.concatenate([own_key[:, columns], own_value[:, columns]], axis=1))
    pairs = jnp.stack(pairs)
    heads = [(mp + k) % n_mp * KV_HEADS // n_mp for k in range(n_mp)]
    shares = around([lax.dynamic_index_in_dim(pairs, h, 0, False) for h in heads])
    arrived, *shares = together(arrived, *shares)
    shares = jnp.stack(shares)
    rows = pick(arrived, slot_source).reshape(tokens, width)

    x = lax.all_gather(rows, "mp", axis=1, tiled=True)
    shares = jnp.stack([shares] + other_chips([shares] * chips))
    native, shares = together(rows, shares)
    other_shares, *plane_rows = together(flip(shares, 1), *from_near(native))
    plane_rows = from_far(native, plane_rows)
    rest = [k for k in range(1, chips) if k not in near]
    far_rows = jnp.concatenate([plane_rows[k] for k in rest])
    plane_rows = jnp.concatenate(plane_rows)

    shares = jnp.stack([shares, other_shares], axis=1).reshape(n_dp * n_mp, share, 2 * dim)
    order = (dp ^ jnp.arange(n_dp))[None, :] * n_mp + ((mp - jnp.arange(n_mp)) % n_mp)[:, None]
    w_kv = pick(shares, order.reshape(-1)).reshape(n_mp * width, 2 * dim)

    x, w_kv, plane_rows, far_rows = together(x, w_kv, plane_rows, far_rows)

    chip_width = n_mp * width // chips
    by_plane = chips == n_mp
    chip_rows = {
        k: lax.dynamic_slice_in_dim(x, (chip ^ k) * chip_width, chip_width, 1)
        for k in range(chips)
        if k in [0] + near or not by_plane
    }
    x, chip_rows = lax.optimization_barrier((x, chip_rows))
    near_rows = [flip(chip_rows[k], 2 * k) for k in near]

    def along(block, steps):
        pairs = [
            (d * n_mp + d // 2 + a, d * n_mp + d // 2 + b)
            for d in range(n_dp)
            for a, b in steps
            if 0 <= d // 2 + a < n_mp and 0 <= d // 2 + b < n_mp
        ]
        return lax.ppermute(block, ("dp", "mp"), pairs)

    if by_plane:
        near_rows += [along(far_rows, [(0, 1)]), along(far_rows, [(0, -1)])]

    factor = multiplicity.astype(F32) * slot_weight / length
    d_out = (cotangent.astype(F32) * factor[:, None, None]).astype(BF16).astype(F32)
    attended, d_query, d_kv = attend(
        x,
        w_query,
        w_kv,
        d_out.reshape(tokens, query_cols),
        query_gain[None, :],
        key_gain[None, :],
        length,
        key_cols // n_dp,
    )
    attended, d_query, d_kv = [value.astype(BF16) for value in (attended, d_query, d_kv)]
    d_query, d_kv, *near_rows = together(d_query, d_kv, *near_rows)
    if by_plane:
        above, below = near_rows[len(near) :]
        hops = [jnp.where(mp > chip, above, below)]
        if n_mp > 2:
            hops.append(along(hops[0], [(1, 2), (-1, -2)]))

    d_all = [d_query] + other_chips([d_query] * chips)
    spread = jnp.stack(around([d_kv] * n_mp))
    d_near = [d_all[k] for k in near]
    d_near, spread, last = lax.optimization_barrier((d_near, spread, hops[-1] if by_plane else x))
    for k, block in zip(near, d_near):
        d_all[k] = block
    for k, block in zip(near, near_rows):
        chip_rows[k] = block
    if by_plane:
        hops[-1] = last
        for hop in range(3, n_mp):
            hops.append(along(hops[-1], [(hop - 1, hop), (1 - hop, -hop)]))
        for hop, block in enumerate(hops, 1):
            far_rows = jnp.where(jnp.abs(mp - chip) == hop, block, far_rows)
        chip_rows.update(zip(rest, jnp.split(far_rows, len(rest))))
    else:
        chip_rows.update({k: flip(chip_rows[k], 2 * k) for k in rest})
    half = chip_width // 2
    early = [0] + near
    late = [k for k in range(chips) if k not in early]

    def product(some, which):
        mine = jnp.concatenate([chip_rows[k] for k in some])
        mine = lax.dynamic_slice_in_dim(mine, which * half, half, 1)
        theirs = jnp.concatenate([d_all[k] for k in some])
        return jnp.einsum("td,tc->dc", mine, theirs, preferred_element_type=F32)

    other = flip((product(early, 1 - core) + product(late, 1 - core)).astype(BF16), 1)
    grad_query = product(late, core) + (product(early, core) + other.astype(F32))

    if n_mp > KV_HEADS:
        spread = pick(spread, (mp - jnp.arange(n_mp)) % n_mp)
        spread = spread.reshape(KV_HEADS, n_mp // KV_HEADS, tokens, 2 * dim)
        spread = jnp.sum(spread.astype(F32), axis=1).astype(BF16)
        spread_at = lambda index: index
    else:
        spread_at = lambda index: (mp - index) % n_mp
    chip_cols = 2 * key_cols // chips
    if chip_cols != 2 * dim:
        spread = spread.reshape(KV_HEADS, tokens, chips // KV_HEADS, chip_cols)
        spread = spread.transpose(0, 2, 1, 3).reshape(chips, tokens, chip_cols)
    kv_all = [lax.dynamic_index_in_dim(spread, spread_at(chip ^ k), 0, False) for k in range(chips)]
    kv_all = jnp.stack([kv_all[0]] + other_chips(kv_all)).reshape(chips * tokens, chip_cols)
    partial = jnp.einsum("td,tc->dc", plane_rows, kv_all, preferred_element_type=F32)
    mine, theirs = partial[:, : chip_cols // 2], partial[:, chip_cols // 2 :]
    mine, theirs = jnp.where(core == 0, mine, theirs), jnp.where(core == 0, theirs, mine)
    grad_kv = mine + flip(theirs.astype(BF16), 1).astype(F32)
    device_cols = chip_cols // 4

    return (
        attended.reshape(slots, length, query_cols),
        grad_query,
        grad_kv[:, :device_cols],
        grad_kv[:, device_cols:],
    )


def solution(mesh):
    return jax.shard_map(
        functools.partial(local, mesh.shape["dp"], mesh.shape["mp"]),
        mesh=mesh,
        in_specs=(
            P("dp", None, "mp"),
            P("dp", None),
            P("dp"),
            P("dp"),
            P("dp"),
            P("dp", None, "mp"),
            P(None, "mp"),
            P("mp", None),
            P("mp", None),
            P(),
            P(),
        ),
        out_specs=(P("dp", None, "mp"), P("dp", "mp"), P("mp", "dp"), P("mp", "dp")),
        check_vma=False,
    )
```

```python
import functools
import math

import jax
import jax.numpy as jnp
from jax import lax
from jax.experimental import pallas as pl
from jax.experimental.pallas import tpu as pltpu
from jax.sharding import PartitionSpec as P

HEADS = 32
KV_HEADS = 4
F32 = jnp.float32
BF16 = jnp.bfloat16


def dot(a, b, contract):
    return lax.dot_general(a, b, ((contract[0], contract[1]), ((), ())), preferred_element_type=F32)


def rms_back(values, inverse, gain, grad_out):
    scaled = grad_out * gain
    inner = jnp.mean(values * scaled, axis=-1, keepdims=True)
    return inverse * scaled - values * (inverse * inverse * inverse) * inner


def attend_tile(query, key, value, d_out, query_gain, key_gain, length):
    tokens, dim = key.shape
    heads = query.shape[1] // dim
    scale = 1.0 / math.sqrt(dim)

    def stack(wide):
        return jnp.concatenate([wide[:, h * dim : (h + 1) * dim] for h in range(heads)], axis=0)

    def unstack(tall):
        return jnp.concatenate(
            [tall[h * tokens : (h + 1) * tokens] for h in range(heads)], axis=1
        )

    query = stack(query)
    q_inverse = lax.rsqrt(jnp.mean(query * query, axis=-1, keepdims=True) + 1e-06)
    q_half = (query * q_inverse * query_gain).astype(BF16)
    k_inverse = lax.rsqrt(jnp.mean(key * key, axis=-1, keepdims=True) + 1e-06)
    k_half = (key * k_inverse * key_gain).astype(BF16)
    v_half = value.astype(BF16)
    out_half = stack(d_out).astype(BF16)

    shape = (tokens, tokens)
    row = lax.broadcasted_iota(jnp.int32, shape, 0)
    col = lax.broadcasted_iota(jnp.int32, shape, 1)
    size = jnp.full(shape, length, jnp.int32)
    allowed = (row >= col) & (lax.div(row, size) == lax.div(col, size))
    allowed = jnp.concatenate([allowed] * heads, axis=0)

    scores = dot(q_half, k_half, ((1,), (1,))) * scale
    scores = jnp.where(allowed, scores, -1e30)
    raised = jnp.exp(scores - jnp.max(scores, axis=-1, keepdims=True))
    probs = raised / jnp.sum(raised, axis=-1, keepdims=True)
    p_half = probs.astype(BF16)
    attended = dot(p_half, v_half, ((1,), (0,)))
    d_probs = dot(out_half, v_half, ((1,), (1,)))
    d_value = dot(p_half, out_half, ((0,), (0,)))
    inner = jnp.sum(d_probs * probs, axis=-1, keepdims=True)
    score_half = (probs * (d_probs - inner) * scale).astype(BF16)
    d_qnorm = dot(score_half, k_half, ((1,), (0,)))
    d_knorm = dot(score_half, q_half, ((0,), (0,)))
    d_query = rms_back(query, q_inverse, query_gain, d_qnorm)
    d_key = rms_back(key, k_inverse, key_gain, d_knorm)
    return (
        unstack(attended),
        unstack(d_query),
        d_key,
        d_value,
    )


def attend_kernel(
    length,
    device_cols,
    x_ref,
    wq_ref,
    wkv_ref,
    d_out_ref,
    query_gain_ref,
    key_gain_ref,
    attended_ref,
    dq_ref,
    dkv_ref,
    query_ref,
    kv_ref,
):
    step = pl.program_id(0)
    x = x_ref[...]
    query_part = jnp.dot(x, wq_ref[...], preferred_element_type=F32)
    kv_part = jnp.dot(x, wkv_ref[...], preferred_element_type=F32)

    @pl.when(step == 0)
    def _():
        query_ref[...] = query_part
        kv_ref[...] = kv_part

    @pl.when(step > 0)
    def _():
        query_ref[...] += query_part
        kv_ref[...] += kv_part

    @pl.when(step == pl.num_programs(0) - 1)
    def _():
        tokens = query_ref.shape[0]
        dim = query_gain_ref.shape[1]
        tile = min(tokens, max(1, 128 // length) * length)
        for start in range(0, tokens, tile):
            rows = slice(start, start + tile)
            attended, d_query, d_key, d_value = attend_tile(
                query_ref[rows, :],
                kv_ref[rows, :dim],
                kv_ref[rows, dim:],
                d_out_ref[rows, :],
                query_gain_ref[...],
                key_gain_ref[...],
                length,
            )
            attended_ref[rows, :] = attended
            dq_ref[rows, :] = d_query
            for first in range(0, dim, device_cols):
                columns = slice(first, first + device_cols)
                pair = jnp.concatenate([d_key[:, columns], d_value[:, columns]], axis=1)
                dkv_ref[rows, 2 * first : 2 * first + 2 * device_cols] = pair


def attend(x, w_query, w_kv, d_out, query_gain, key_gain, length, device_cols):
    tokens, depth = x.shape
    cols = w_query.shape[1]
    kv_cols = w_kv.shape[1]
    block = depth // 4
    whole = lambda shape: pl.BlockSpec(shape, lambda b: (0, 0))
    return pl.pallas_call(
        functools.partial(attend_kernel, length, device_cols),
        grid=(depth // block,),
        in_specs=[
            pl.BlockSpec((tokens, block), lambda b: (0, b)),
            pl.BlockSpec((block, cols), lambda b: (b, 0)),
            pl.BlockSpec((block, kv_cols), lambda b: (b, 0)),
            whole(d_out.shape),
            whole(query_gain.shape),
            whole(key_gain.shape),
        ],
        out_specs=[whole((tokens, cols)), whole((tokens, cols)), whole((tokens, kv_cols))],
        out_shape=[
            jax.ShapeDtypeStruct((tokens, cols), F32),
            jax.ShapeDtypeStruct((tokens, cols), F32),
            jax.ShapeDtypeStruct((tokens, kv_cols), F32),
        ],
        scratch_shapes=[pltpu.VMEM((tokens, cols), F32), pltpu.VMEM((tokens, kv_cols), F32)],
        compiler_params=pltpu.CompilerParams(vmem_limit_bytes=40 * 1024 * 1024),
        cost_estimate=pl.CostEstimate(
            flops=10 * tokens * depth * (cols + kv_cols),
            bytes_accessed=8 * w_query.size,
            transcendentals=tokens * cols,
        ),
    )(x, w_query, w_kv, d_out, query_gain, key_gain)


def together(*values):
    return lax.optimization_barrier(values)


def pick(array, index):
    return array.at[index].get(mode="promise_in_bounds")


def local(
    n_dp,
    n_mp,
    pool,
    send_table,
    slot_source,
    multiplicity,
    slot_weight,
    cotangent,
    w_query,
    w_key,
    w_value,
    query_gain,
    key_gain,
):
    slots = slot_source.shape[0]
    length = pool.shape[1]
    width = pool.shape[2]
    query_cols = w_query.shape[1]
    key_cols = w_key.shape[1]
    dim = query_gain.shape[0]
    tokens = slots * length
    chips = n_dp // 2
    dp = lax.axis_index("dp")
    mp = lax.axis_index("mp")
    chip, core = dp // 2, dp % 2

    def flip(block, bits):
        return lax.ppermute(block, "dp", [(i, i ^ bits) for i in range(n_dp)])

    def other_chips(blocks):
        return [flip(blocks[k], 2 * k) for k in range(1, chips)]

    def around(blocks):
        return [blocks[0]] + [
            lax.ppermute(blocks[k], "mp", [(i, (i + k) % n_mp) for i in range(n_mp)])
            for k in range(1, n_mp)
        ]

    near = [1 << b for b in range(chips.bit_length() - 1)]

    def from_near(block):
        return [flip(block, 2 * k) for k in near]

    def from_far(block, arrived):
        arrived = dict(zip(near, arrived))
        middle = block.shape[0] // 2
        blocks = [block]
        for k in range(1, chips):
            bits = [n for n in near if k & n]
            if len(bits) == 1:
                blocks.append(arrived[k])
            elif len(bits) == 2:
                first = flip(arrived[bits[0]][:middle], 2 * bits[1])
                second = flip(arrived[bits[1]][middle:], 2 * bits[0])
                blocks.append(jnp.concatenate([first, second]))
            else:
                blocks.append(flip(block, 2 * k))
        return blocks

    outgoing = pick(pool, jnp.maximum(send_table[0], 0))
    outgoing, w_key, w_value = together(outgoing, w_key, w_value)
    arrived = lax.all_to_all(outgoing, "dp", split_axis=0, concat_axis=0, tiled=True)

    share = width // n_dp
    own_key = lax.dynamic_slice_in_dim(w_key, dp * share, share, 0)
    own_value = lax.dynamic_slice_in_dim(w_value, dp * share, share, 0)
    pairs = []
    for head in range(KV_HEADS):
        columns = slice(head * dim, (head + 1) * dim)
        pairs.append(jnp.concatenate([own_key[:, columns], own_value[:, columns]], axis=1))
    pairs = jnp.stack(pairs)
    heads = [(mp + k) % n_mp * KV_HEADS // n_mp for k in range(n_mp)]
    pairs = [lax.dynamic_index_in_dim(pairs, h, 0, False) for h in heads]
    arrived, pairs = lax.optimization_barrier((arrived, pairs))
    shares = jnp.stack(around(pairs))
    rows = pick(arrived, slot_source).reshape(tokens, width)

    x = lax.all_gather(rows, "mp", axis=1, tiled=True)
    shares = jnp.stack([shares] + other_chips([shares] * chips))
    native, shares = together(rows, shares)
    other_shares, *plane_rows = together(flip(shares, 1), *from_near(native))
    plane_rows = from_far(native, plane_rows)
    rest = [k for k in range(1, chips) if k not in near]
    by_plane = chips == n_mp
    cut = tokens * 3 // 4 if by_plane else 0
    far_rows = jnp.concatenate([plane_rows[k][:cut] for k in rest])
    plane_rows = jnp.concatenate(plane_rows)

    shares = jnp.stack([shares, other_shares], axis=1).reshape(n_dp * n_mp, share, 2 * dim)
    order = (dp ^ jnp.arange(n_dp))[None, :] * n_mp + ((mp - jnp.arange(n_mp)) % n_mp)[:, None]
    w_kv = pick(shares, order.reshape(-1)).reshape(n_mp * width, 2 * dim)

    x, w_kv, plane_rows, far_rows = together(x, w_kv, plane_rows, far_rows)

    chip_width = n_mp * width // chips
    chip_rows = {
        k: lax.dynamic_slice_in_dim(
            x[cut:] if k in rest else x, (chip ^ k) * chip_width, chip_width, 1
        )
        for k in range(chips)
    }
    x, chip_rows = lax.optimization_barrier((x, chip_rows))
    near_rows = [flip(chip_rows[k], 2 * k) for k in near]

    def along(block, steps):
        pairs = [
            (d * n_mp + d // 2 + a, d * n_mp + d // 2 + b)
            for d in range(n_dp)
            for a, b in steps
            if 0 <= d // 2 + a < n_mp and 0 <= d // 2 + b < n_mp
        ]
        return lax.ppermute(block, ("dp", "mp"), pairs)

    if by_plane:
        near_rows += [along(far_rows, [(0, 1)]), along(far_rows, [(0, -1)])]

    factor = multiplicity.astype(F32) * slot_weight / length
    d_out = (cotangent.astype(F32) * factor[:, None, None]).astype(BF16).astype(F32)
    attended, d_query, d_kv = attend(
        x,
        w_query,
        w_kv,
        d_out.reshape(tokens, query_cols),
        query_gain[None, :],
        key_gain[None, :],
        length,
        key_cols // n_dp,
    )
    attended, d_query, d_kv = [value.astype(BF16) for value in (attended, d_query, d_kv)]
    d_query, d_kv, *near_rows = together(d_query, d_kv, *near_rows)
    if by_plane:
        above, below = near_rows[len(near) :]
        hops = [jnp.where(mp > chip, above, below)]
        if n_mp > 2:
            hops.append(along(hops[0], [(1, 2), (-1, -2)]))

    d_all = [d_query] + other_chips([d_query] * chips)
    spread = jnp.stack(around([d_kv] * n_mp))
    d_near = [d_all[k] for k in near]
    direct = [flip(chip_rows[k], 2 * k) for k in rest]
    d_near, spread, direct, last = lax.optimization_barrier(
        (d_near, spread, direct, hops[-1] if by_plane else x)
    )
    for k, block in zip(near, d_near):
        d_all[k] = block
    for k, block in zip(near, near_rows):
        chip_rows[k] = block
    if by_plane:
        hops[-1] = last
        for hop in range(3, n_mp):
            hops.append(along(hops[-1], [(hop - 1, hop), (1 - hop, -hop)]))
        for hop, block in enumerate(hops, 1):
            far_rows = jnp.where(jnp.abs(mp - chip) == hop, block, far_rows)
        direct = [
            jnp.concatenate(parts) for parts in zip(jnp.split(far_rows, len(rest)), direct)
        ]
    chip_rows.update(zip(rest, direct))
    half = chip_width // 2
    early = [0] + near
    late = [k for k in range(chips) if k not in early]

    def product(some, which):
        mine = jnp.concatenate([chip_rows[k] for k in some])
        mine = lax.dynamic_slice_in_dim(mine, which * half, half, 1)
        theirs = jnp.concatenate([d_all[k] for k in some])
        return jnp.einsum("td,tc->dc", mine, theirs, preferred_element_type=F32)

    other = flip((product(early, 1 - core) + product(late, 1 - core)).astype(BF16), 1)
    grad_query = product(late, core) + (product(early, core) + other.astype(F32))

    if n_mp > KV_HEADS:
        spread = pick(spread, (mp - jnp.arange(n_mp)) % n_mp)
        spread = spread.reshape(KV_HEADS, n_mp // KV_HEADS, tokens, 2 * dim)
        spread = jnp.sum(spread.astype(F32), axis=1).astype(BF16)
        spread_at = lambda index: index
    else:
        spread_at = lambda index: (mp - index) % n_mp
    chip_cols = 2 * key_cols // chips
    if chip_cols != 2 * dim:
        spread = spread.reshape(KV_HEADS, tokens, chips // KV_HEADS, chip_cols)
        spread = spread.transpose(0, 2, 1, 3).reshape(chips, tokens, chip_cols)
    kv_all = [lax.dynamic_index_in_dim(spread, spread_at(chip ^ k), 0, False) for k in range(chips)]
    kv_all = jnp.stack([kv_all[0]] + other_chips(kv_all)).reshape(chips * tokens, chip_cols)
    partial = jnp.einsum("td,tc->dc", plane_rows, kv_all, preferred_element_type=F32)
    mine, theirs = partial[:, : chip_cols // 2], partial[:, chip_cols // 2 :]
    mine, theirs = jnp.where(core == 0, mine, theirs), jnp.where(core == 0, theirs, mine)
    grad_kv = mine + flip(theirs.astype(BF16), 1).astype(F32)
    device_cols = chip_cols // 4

    return (
        attended.reshape(slots, length, query_cols),
        grad_query,
        grad_kv[:, :device_cols],
        grad_kv[:, device_cols:],
    )


def solution(mesh):
    return jax.shard_map(
        functools.partial(local, mesh.shape["dp"], mesh.shape["mp"]),
        mesh=mesh,
        in_specs=(
            P("dp", None, "mp"),
            P("dp", None),
            P("dp"),
            P("dp"),
            P("dp"),
            P("dp", None, "mp"),
            P(None, "mp"),
            P("mp", None),
            P("mp", None),
            P(),
            P(),
        ),
        out_specs=(P("dp", None, "mp"), P("dp", "mp"), P("mp", "dp"), P("mp", "dp")),
        check_vma=False,
    )
```

```python
import functools
import math

import jax
import jax.numpy as jnp
from jax import lax
from jax.experimental import pallas as pl
from jax.experimental.pallas import tpu as pltpu
from jax.sharding import PartitionSpec as P

HEADS = 32
KV_HEADS = 4
F32 = jnp.float32
BF16 = jnp.bfloat16


def dot(a, b, contract):
    return lax.dot_general(a, b, ((contract[0], contract[1]), ((), ())), preferred_element_type=F32)


def rms_back(values, inverse, gain, grad_out):
    scaled = grad_out * gain
    inner = jnp.mean(values * scaled, axis=-1, keepdims=True)
    return inverse * scaled - values * (inverse * inverse * inverse) * inner


def attend_tile(query, key, value, d_out, query_gain, key_gain, length):
    tokens, dim = key.shape
    heads = query.shape[1] // dim
    scale = 1.0 / math.sqrt(dim)

    def stack(wide):
        return jnp.concatenate([wide[:, h * dim : (h + 1) * dim] for h in range(heads)], axis=0)

    def unstack(tall):
        return jnp.concatenate(
            [tall[h * tokens : (h + 1) * tokens] for h in range(heads)], axis=1
        )

    query = stack(query)
    q_inverse = lax.rsqrt(jnp.mean(query * query, axis=-1, keepdims=True) + 1e-06)
    q_half = (query * q_inverse * query_gain).astype(BF16)
    k_inverse = lax.rsqrt(jnp.mean(key * key, axis=-1, keepdims=True) + 1e-06)
    k_half = (key * k_inverse * key_gain).astype(BF16)
    v_half = value.astype(BF16)
    out_half = stack(d_out).astype(BF16)

    shape = (tokens, tokens)
    row = lax.broadcasted_iota(jnp.int32, shape, 0)
    col = lax.broadcasted_iota(jnp.int32, shape, 1)
    size = jnp.full(shape, length, jnp.int32)
    allowed = (row >= col) & (lax.div(row, size) == lax.div(col, size))
    allowed = jnp.concatenate([allowed] * heads, axis=0)

    scores = dot(q_half, k_half, ((1,), (1,))) * scale
    scores = jnp.where(allowed, scores, -1e30)
    raised = jnp.exp(scores - jnp.max(scores, axis=-1, keepdims=True))
    probs = raised / jnp.sum(raised, axis=-1, keepdims=True)
    p_half = probs.astype(BF16)
    attended = dot(p_half, v_half, ((1,), (0,)))
    d_probs = dot(out_half, v_half, ((1,), (1,)))
    d_value = dot(p_half, out_half, ((0,), (0,)))
    inner = jnp.sum(d_probs * probs, axis=-1, keepdims=True)
    score_half = (probs * (d_probs - inner) * scale).astype(BF16)
    d_qnorm = dot(score_half, k_half, ((1,), (0,)))
    d_knorm = dot(score_half, q_half, ((0,), (0,)))
    d_query = rms_back(query, q_inverse, query_gain, d_qnorm)
    d_key = rms_back(key, k_inverse, key_gain, d_knorm)
    return (
        unstack(attended),
        unstack(d_query),
        d_key,
        d_value,
    )


def attend_kernel(
    length,
    device_cols,
    x_ref,
    wq_ref,
    wkv_ref,
    d_out_ref,
    query_gain_ref,
    key_gain_ref,
    attended_ref,
    dq_ref,
    dkv_ref,
    query_ref,
    kv_ref,
):
    step = pl.program_id(0)
    x = x_ref[...]
    query_part = jnp.dot(x, wq_ref[...], preferred_element_type=F32)
    kv_part = jnp.dot(x, wkv_ref[...], preferred_element_type=F32)

    @pl.when(step == 0)
    def _():
        query_ref[...] = query_part
        kv_ref[...] = kv_part

    @pl.when(step > 0)
    def _():
        query_ref[...] += query_part
        kv_ref[...] += kv_part

    @pl.when(step == pl.num_programs(0) - 1)
    def _():
        tokens = query_ref.shape[0]
        dim = query_gain_ref.shape[1]
        tile = min(tokens, max(1, 128 // length) * length)
        for start in range(0, tokens, tile):
            rows = slice(start, start + tile)
            attended, d_query, d_key, d_value = attend_tile(
                query_ref[rows, :],
                kv_ref[rows, :dim],
                kv_ref[rows, dim:],
                d_out_ref[rows, :],
                query_gain_ref[...],
                key_gain_ref[...],
                length,
            )
            attended_ref[rows, :] = attended
            dq_ref[rows, :] = d_query
            for first in range(0, dim, device_cols):
                columns = slice(first, first + device_cols)
                pair = jnp.concatenate([d_key[:, columns], d_value[:, columns]], axis=1)
                dkv_ref[rows, 2 * first : 2 * first + 2 * device_cols] = pair


def attend(x, w_query, w_kv, d_out, query_gain, key_gain, length, device_cols):
    tokens, depth = x.shape
    cols = w_query.shape[1]
    kv_cols = w_kv.shape[1]
    block = depth // 4
    whole = lambda shape: pl.BlockSpec(shape, lambda b: (0, 0))
    return pl.pallas_call(
        functools.partial(attend_kernel, length, device_cols),
        grid=(depth // block,),
        in_specs=[
            pl.BlockSpec((tokens, block), lambda b: (0, b)),
            pl.BlockSpec((block, cols), lambda b: (b, 0)),
            pl.BlockSpec((block, kv_cols), lambda b: (b, 0)),
            whole(d_out.shape),
            whole(query_gain.shape),
            whole(key_gain.shape),
        ],
        out_specs=[whole((tokens, cols)), whole((tokens, cols)), whole((tokens, kv_cols))],
        out_shape=[
            jax.ShapeDtypeStruct((tokens, cols), F32),
            jax.ShapeDtypeStruct((tokens, cols), F32),
            jax.ShapeDtypeStruct((tokens, kv_cols), F32),
        ],
        scratch_shapes=[pltpu.VMEM((tokens, cols), F32), pltpu.VMEM((tokens, kv_cols), F32)],
        compiler_params=pltpu.CompilerParams(vmem_limit_bytes=40 * 1024 * 1024),
        cost_estimate=pl.CostEstimate(
            flops=10 * tokens * depth * (cols + kv_cols),
            bytes_accessed=8 * w_query.size,
            transcendentals=tokens * cols,
        ),
    )(x, w_query, w_kv, d_out, query_gain, key_gain)


def together(*values):
    return lax.optimization_barrier(values)


def pick(array, index):
    return array.at[index].get(mode="promise_in_bounds")


def local(
    n_dp,
    n_mp,
    pool,
    send_table,
    slot_source,
    multiplicity,
    slot_weight,
    cotangent,
    w_query,
    w_key,
    w_value,
    query_gain,
    key_gain,
):
    slots = slot_source.shape[0]
    length = pool.shape[1]
    width = pool.shape[2]
    query_cols = w_query.shape[1]
    key_cols = w_key.shape[1]
    dim = query_gain.shape[0]
    tokens = slots * length
    chips = n_dp // 2
    dp = lax.axis_index("dp")
    mp = lax.axis_index("mp")
    chip, core = dp // 2, dp % 2

    def flip(block, bits):
        return lax.ppermute(block, "dp", [(i, i ^ bits) for i in range(n_dp)])

    def other_chips(blocks):
        return [flip(blocks[k], 2 * k) for k in range(1, chips)]

    def around(blocks):
        return [blocks[0]] + [
            lax.ppermute(blocks[k], "mp", [(i, (i + k) % n_mp) for i in range(n_mp)])
            for k in range(1, n_mp)
        ]

    near = [1 << b for b in range(chips.bit_length() - 1)]

    def from_near(block):
        return [flip(block, 2 * k) for k in near]

    def from_far(block, arrived):
        arrived = dict(zip(near, arrived))
        middle = block.shape[0] // 2
        blocks = [block]
        for k in range(1, chips):
            bits = [n for n in near if k & n]
            if len(bits) == 1:
                blocks.append(arrived[k])
            elif len(bits) == 2:
                first = flip(arrived[bits[0]][:middle], 2 * bits[1])
                second = flip(arrived[bits[1]][middle:], 2 * bits[0])
                blocks.append(jnp.concatenate([first, second]))
            else:
                blocks.append(flip(block, 2 * k))
        return blocks

    outgoing = pick(pool, jnp.maximum(send_table[0], 0))
    outgoing, w_key, w_value = together(outgoing, w_key, w_value)
    arrived = lax.all_to_all(outgoing, "dp", split_axis=0, concat_axis=0, tiled=True)

    share = width // n_dp
    own_key = lax.dynamic_slice_in_dim(w_key, dp * share, share, 0)
    own_value = lax.dynamic_slice_in_dim(w_value, dp * share, share, 0)
    pairs = []
    for head in range(KV_HEADS):
        columns = slice(head * dim, (head + 1) * dim)
        pairs.append(jnp.concatenate([own_key[:, columns], own_value[:, columns]], axis=1))
    pairs = jnp.stack(pairs)
    heads = [(mp + k) % n_mp * KV_HEADS // n_mp for k in range(n_mp)]
    shares = around([lax.dynamic_index_in_dim(pairs, h, 0, False) for h in heads])
    rows = pick(arrived, slot_source).reshape(tokens, width)
    rows, *shares = together(rows, *shares)
    shares = jnp.stack(shares)

    x = lax.all_gather(rows, "mp", axis=1, tiled=True)
    shares = jnp.stack([shares] + other_chips([shares] * chips))
    native, shares = together(rows, shares)
    other_shares, *plane_rows = together(flip(shares, 1), *from_near(native))
    plane_rows = from_far(native, plane_rows)
    rest = [k for k in range(1, chips) if k not in near]
    far_rows = jnp.concatenate([plane_rows[k] for k in rest])
    plane_rows = jnp.concatenate(plane_rows)

    shares = jnp.stack([shares, other_shares], axis=1).reshape(n_dp * n_mp, share, 2 * dim)
    order = (dp ^ jnp.arange(n_dp))[None, :] * n_mp + ((mp - jnp.arange(n_mp)) % n_mp)[:, None]
    w_kv = pick(shares, order.reshape(-1)).reshape(n_mp * width, 2 * dim)

    x, w_kv, plane_rows, far_rows = together(x, w_kv, plane_rows, far_rows)

    chip_width = n_mp * width // chips
    by_plane = chips == n_mp
    chip_rows = {
        k: lax.dynamic_slice_in_dim(x, (chip ^ k) * chip_width, chip_width, 1)
        for k in range(chips)
        if k in [0] + near or not by_plane
    }
    x, chip_rows = lax.optimization_barrier((x, chip_rows))
    near_rows = [flip(chip_rows[k], 2 * k) for k in near]

    def along(block, steps):
        pairs = [
            (d * n_mp + d // 2 + a, d * n_mp + d // 2 + b)
            for d in range(n_dp)
            for a, b in steps
            if 0 <= d // 2 + a < n_mp and 0 <= d // 2 + b < n_mp
        ]
        return lax.ppermute(block, ("dp", "mp"), pairs)

    if by_plane:
        near_rows += [along(far_rows, [(0, 1)]), along(far_rows, [(0, -1)])]

    factor = multiplicity.astype(F32) * slot_weight / length
    d_out = (cotangent.astype(F32) * factor[:, None, None]).astype(BF16).astype(F32)
    attended, d_query, d_kv = attend(
        x,
        w_query,
        w_kv,
        d_out.reshape(tokens, query_cols),
        query_gain[None, :],
        key_gain[None, :],
        length,
        key_cols // n_dp,
    )
    attended, d_query, d_kv = [value.astype(BF16) for value in (attended, d_query, d_kv)]
    d_query, d_kv, *near_rows = together(d_query, d_kv, *near_rows)
    if by_plane:
        above, below = near_rows[len(near) :]
        hops = [jnp.where(mp > chip, above, below)]
        if n_mp > 2:
            hops.append(along(hops[0], [(1, 2), (-1, -2)]))

    d_all = [d_query] + other_chips([d_query] * chips)
    spread = jnp.stack(around([d_kv] * n_mp))
    d_near = [d_all[k] for k in near]
    d_near, spread, last = lax.optimization_barrier((d_near, spread, hops[-1] if by_plane else x))
    for k, block in zip(near, d_near):
        d_all[k] = block
    for k, block in zip(near, near_rows):
        chip_rows[k] = block
    if by_plane:
        hops[-1] = last
        for hop in range(3, n_mp):
            hops.append(along(hops[-1], [(hop - 1, hop), (1 - hop, -hop)]))
        for hop, block in enumerate(hops, 1):
            far_rows = jnp.where(jnp.abs(mp - chip) == hop, block, far_rows)
        chip_rows.update(zip(rest, jnp.split(far_rows, len(rest))))
    else:
        chip_rows.update({k: flip(chip_rows[k], 2 * k) for k in rest})
    half = chip_width // 2
    early = [0] + near
    late = [k for k in range(chips) if k not in early]

    def product(some, which):
        mine = jnp.concatenate([chip_rows[k] for k in some])
        mine = lax.dynamic_slice_in_dim(mine, which * half, half, 1)
        theirs = jnp.concatenate([d_all[k] for k in some])
        return jnp.einsum("td,tc->dc", mine, theirs, preferred_element_type=F32)

    other = flip((product(early, 1 - core) + product(late, 1 - core)).astype(BF16), 1)
    grad_query = product(late, core) + (product(early, core) + other.astype(F32))

    if n_mp > KV_HEADS:
        spread = pick(spread, (mp - jnp.arange(n_mp)) % n_mp)
        spread = spread.reshape(KV_HEADS, n_mp // KV_HEADS, tokens, 2 * dim)
        spread = jnp.sum(spread.astype(F32), axis=1).astype(BF16)
        spread_at = lambda index: index
    else:
        spread_at = lambda index: (mp - index) % n_mp
    chip_cols = 2 * key_cols // chips
    if chip_cols != 2 * dim:
        spread = spread.reshape(KV_HEADS, tokens, chips // KV_HEADS, chip_cols)
        spread = spread.transpose(0, 2, 1, 3).reshape(chips, tokens, chip_cols)
    kv_all = [lax.dynamic_index_in_dim(spread, spread_at(chip ^ k), 0, False) for k in range(chips)]
    kv_all = jnp.stack([kv_all[0]] + other_chips(kv_all)).reshape(chips * tokens, chip_cols)
    partial = jnp.einsum("td,tc->dc", plane_rows, kv_all, preferred_element_type=F32)
    mine, theirs = partial[:, : chip_cols // 2], partial[:, chip_cols // 2 :]
    mine, theirs = jnp.where(core == 0, mine, theirs), jnp.where(core == 0, theirs, mine)
    grad_kv = mine + flip(theirs.astype(BF16), 1).astype(F32)
    device_cols = chip_cols // 4

    return (
        attended.reshape(slots, length, query_cols),
        grad_query,
        grad_kv[:, :device_cols],
        grad_kv[:, device_cols:],
    )


def solution(mesh):
    return jax.shard_map(
        functools.partial(local, mesh.shape["dp"], mesh.shape["mp"]),
        mesh=mesh,
        in_specs=(
            P("dp", None, "mp"),
            P("dp", None),
            P("dp"),
            P("dp"),
            P("dp"),
            P("dp", None, "mp"),
            P(None, "mp"),
            P("mp", None),
            P("mp", None),
            P(),
            P(),
        ),
        out_specs=(P("dp", None, "mp"), P("dp", "mp"), P("mp", "dp"), P("mp", "dp")),
        check_vma=False,
    )
```

```python
import functools
import math

import jax
import jax.numpy as jnp
from jax import lax
from jax.experimental import pallas as pl
from jax.experimental.pallas import tpu as pltpu
from jax.sharding import PartitionSpec as P

HEADS = 32
KV_HEADS = 4
F32 = jnp.float32
BF16 = jnp.bfloat16


def dot(a, b, contract):
    return lax.dot_general(a, b, ((contract[0], contract[1]), ((), ())), preferred_element_type=F32)


def rms_back(values, inverse, gain, grad_out):
    scaled = grad_out * gain
    inner = jnp.mean(values * scaled, axis=-1, keepdims=True)
    return inverse * scaled - values * (inverse * inverse * inverse) * inner


def attend_tile(query, key, value, d_out, query_gain, key_gain, length):
    tokens, dim = key.shape
    heads = query.shape[1] // dim
    scale = 1.0 / math.sqrt(dim)

    def stack(wide):
        return jnp.concatenate([wide[:, h * dim : (h + 1) * dim] for h in range(heads)], axis=0)

    def unstack(tall):
        return jnp.concatenate(
            [tall[h * tokens : (h + 1) * tokens] for h in range(heads)], axis=1
        )

    query = stack(query)
    q_inverse = lax.rsqrt(jnp.mean(query * query, axis=-1, keepdims=True) + 1e-06)
    q_half = (query * q_inverse * query_gain).astype(BF16)
    k_inverse = lax.rsqrt(jnp.mean(key * key, axis=-1, keepdims=True) + 1e-06)
    k_half = (key * k_inverse * key_gain).astype(BF16)
    v_half = value.astype(BF16)
    out_half = stack(d_out).astype(BF16)

    shape = (tokens, tokens)
    row = lax.broadcasted_iota(jnp.int32, shape, 0)
    col = lax.broadcasted_iota(jnp.int32, shape, 1)
    size = jnp.full(shape, length, jnp.int32)
    allowed = (row >= col) & (lax.div(row, size) == lax.div(col, size))
    allowed = jnp.concatenate([allowed] * heads, axis=0)

    scores = dot(q_half, k_half, ((1,), (1,))) * scale
    scores = jnp.where(allowed, scores, -1e30)
    raised = jnp.exp(scores - jnp.max(scores, axis=-1, keepdims=True))
    probs = raised / jnp.sum(raised, axis=-1, keepdims=True)
    p_half = probs.astype(BF16)
    attended = dot(p_half, v_half, ((1,), (0,)))
    d_probs = dot(out_half, v_half, ((1,), (1,)))
    d_value = dot(p_half, out_half, ((0,), (0,)))
    inner = jnp.sum(d_probs * probs, axis=-1, keepdims=True)
    score_half = (probs * (d_probs - inner) * scale).astype(BF16)
    d_qnorm = dot(score_half, k_half, ((1,), (0,)))
    d_knorm = dot(score_half, q_half, ((0,), (0,)))
    d_query = rms_back(query, q_inverse, query_gain, d_qnorm)
    d_key = rms_back(key, k_inverse, key_gain, d_knorm)
    return (
        unstack(attended),
        unstack(d_query),
        d_key,
        d_value,
    )


def attend_kernel(
    length,
    device_cols,
    x_ref,
    wq_ref,
    wkv_ref,
    d_out_ref,
    query_gain_ref,
    key_gain_ref,
    attended_ref,
    dq_ref,
    dkv_ref,
    query_ref,
    kv_ref,
):
    step = pl.program_id(0)
    x = x_ref[...]
    query_part = jnp.dot(x, wq_ref[...], preferred_element_type=F32)
    kv_part = jnp.dot(x, wkv_ref[...], preferred_element_type=F32)

    @pl.when(step == 0)
    def _():
        query_ref[...] = query_part
        kv_ref[...] = kv_part

    @pl.when(step > 0)
    def _():
        query_ref[...] += query_part
        kv_ref[...] += kv_part

    @pl.when(step == pl.num_programs(0) - 1)
    def _():
        tokens = query_ref.shape[0]
        dim = query_gain_ref.shape[1]
        tile = min(tokens, max(1, 128 // length) * length)
        for start in range(0, tokens, tile):
            rows = slice(start, start + tile)
            attended, d_query, d_key, d_value = attend_tile(
                query_ref[rows, :],
                kv_ref[rows, :dim],
                kv_ref[rows, dim:],
                d_out_ref[rows, :],
                query_gain_ref[...],
                key_gain_ref[...],
                length,
            )
            attended_ref[rows, :] = attended
            dq_ref[rows, :] = d_query
            for first in range(0, dim, device_cols):
                columns = slice(first, first + device_cols)
                pair = jnp.concatenate([d_key[:, columns], d_value[:, columns]], axis=1)
                dkv_ref[rows, 2 * first : 2 * first + 2 * device_cols] = pair


def attend(x, w_query, w_kv, d_out, query_gain, key_gain, length, device_cols):
    tokens, depth = x.shape
    cols = w_query.shape[1]
    kv_cols = w_kv.shape[1]
    block = depth // 4
    whole = lambda shape: pl.BlockSpec(shape, lambda b: (0, 0))
    return pl.pallas_call(
        functools.partial(attend_kernel, length, device_cols),
        grid=(depth // block,),
        in_specs=[
            pl.BlockSpec((tokens, block), lambda b: (0, b)),
            pl.BlockSpec((block, cols), lambda b: (b, 0)),
            pl.BlockSpec((block, kv_cols), lambda b: (b, 0)),
            whole(d_out.shape),
            whole(query_gain.shape),
            whole(key_gain.shape),
        ],
        out_specs=[whole((tokens, cols)), whole((tokens, cols)), whole((tokens, kv_cols))],
        out_shape=[
            jax.ShapeDtypeStruct((tokens, cols), F32),
            jax.ShapeDtypeStruct((tokens, cols), F32),
            jax.ShapeDtypeStruct((tokens, kv_cols), F32),
        ],
        scratch_shapes=[pltpu.VMEM((tokens, cols), F32), pltpu.VMEM((tokens, kv_cols), F32)],
        compiler_params=pltpu.CompilerParams(vmem_limit_bytes=40 * 1024 * 1024),
        cost_estimate=pl.CostEstimate(
            flops=10 * tokens * depth * (cols + kv_cols),
            bytes_accessed=8 * w_query.size,
            transcendentals=tokens * cols,
        ),
    )(x, w_query, w_kv, d_out, query_gain, key_gain)


def together(*values):
    return lax.optimization_barrier(values)


def pick(array, index):
    return array.at[index].get(mode="promise_in_bounds")


def local(
    n_dp,
    n_mp,
    pool,
    send_table,
    slot_source,
    multiplicity,
    slot_weight,
    cotangent,
    w_query,
    w_key,
    w_value,
    query_gain,
    key_gain,
):
    slots = slot_source.shape[0]
    length = pool.shape[1]
    width = pool.shape[2]
    query_cols = w_query.shape[1]
    key_cols = w_key.shape[1]
    dim = query_gain.shape[0]
    tokens = slots * length
    chips = n_dp // 2
    dp = lax.axis_index("dp")
    mp = lax.axis_index("mp")
    chip, core = dp // 2, dp % 2

    def flip(block, bits):
        return lax.ppermute(block, "dp", [(i, i ^ bits) for i in range(n_dp)])

    def other_chips(blocks):
        return [flip(blocks[k], 2 * k) for k in range(1, chips)]

    def around(blocks):
        return [blocks[0]] + [
            lax.ppermute(blocks[k], "mp", [(i, (i + k) % n_mp) for i in range(n_mp)])
            for k in range(1, n_mp)
        ]

    near = [1 << b for b in range(chips.bit_length() - 1)]

    def from_near(block):
        return [flip(block, 2 * k) for k in near]

    def from_far(block, arrived):
        arrived = dict(zip(near, arrived))
        middle = block.shape[0] // 2
        blocks = [block]
        for k in range(1, chips):
            bits = [n for n in near if k & n]
            if len(bits) == 1:
                blocks.append(arrived[k])
            elif len(bits) == 2:
                first = flip(arrived[bits[0]][:middle], 2 * bits[1])
                second = flip(arrived[bits[1]][middle:], 2 * bits[0])
                blocks.append(jnp.concatenate([first, second]))
            else:
                blocks.append(flip(block, 2 * k))
        return blocks

    outgoing = pick(pool, jnp.maximum(send_table[0], 0))
    outgoing, w_key, w_value = together(outgoing, w_key, w_value)
    arrived = lax.all_to_all(outgoing, "dp", split_axis=0, concat_axis=0, tiled=True)

    share = width // n_dp
    own_key = lax.dynamic_slice_in_dim(w_key, dp * share, share, 0)
    own_value = lax.dynamic_slice_in_dim(w_value, dp * share, share, 0)
    pairs = []
    for head in range(KV_HEADS):
        columns = slice(head * dim, (head + 1) * dim)
        pairs.append(jnp.concatenate([own_key[:, columns], own_value[:, columns]], axis=1))
    pairs = jnp.stack(pairs)
    heads = [(mp + k) % n_mp * KV_HEADS // n_mp for k in range(n_mp)]
    shares = around([lax.dynamic_index_in_dim(pairs, h, 0, False) for h in heads])
    rows = pick(arrived, slot_source).reshape(tokens, width)
    rows, *shares = together(rows, *shares)
    shares = jnp.stack(shares)

    x = lax.all_gather(rows, "mp", axis=1, tiled=True)
    shares = jnp.stack([shares] + other_chips([shares] * chips))
    native, shares = together(rows, shares)
    other_shares, *plane_rows = together(flip(shares, 1), *from_near(native))
    plane_rows = from_far(native, plane_rows)
    rest = [k for k in range(1, chips) if k not in near]
    far_rows = jnp.concatenate([plane_rows[k] for k in rest])
    plane_rows = jnp.concatenate(plane_rows)

    shares = jnp.stack([shares, other_shares], axis=1).reshape(n_dp * n_mp, share, 2 * dim)
    order = (dp ^ jnp.arange(n_dp))[None, :] * n_mp + ((mp - jnp.arange(n_mp)) % n_mp)[:, None]
    w_kv = pick(shares, order.reshape(-1)).reshape(n_mp * width, 2 * dim)

    x, w_kv, plane_rows, far_rows = together(x, w_kv, plane_rows, far_rows)

    chip_width = n_mp * width // chips
    by_plane = chips == n_mp
    chip_rows = {
        k: lax.dynamic_slice_in_dim(x, (chip ^ k) * chip_width, chip_width, 1)
        for k in range(chips)
        if k in [0] + near or not by_plane
    }
    x, chip_rows = lax.optimization_barrier((x, chip_rows))
    near_rows = [flip(chip_rows[k], 2 * k) for k in near]

    def along(block, steps):
        pairs = [
            (d * n_mp + d // 2 + a, d * n_mp + d // 2 + b)
            for d in range(n_dp)
            for a, b in steps
            if 0 <= d // 2 + a < n_mp and 0 <= d // 2 + b < n_mp
        ]
        return lax.ppermute(block, ("dp", "mp"), pairs)

    if by_plane:
        near_rows += [along(far_rows, [(0, 1)]), along(far_rows, [(0, -1)])]

    factor = multiplicity.astype(F32) * slot_weight / length
    d_out = (cotangent.astype(F32) * factor[:, None, None]).astype(BF16).astype(F32)
    attended, d_query, d_kv = attend(
        x,
        w_query,
        w_kv,
        d_out.reshape(tokens, query_cols),
        query_gain[None, :],
        key_gain[None, :],
        length,
        key_cols // n_dp,
    )
    attended, d_query, d_kv = [value.astype(BF16) for value in (attended, d_query, d_kv)]
    d_query, d_kv, *near_rows = together(d_query, d_kv, *near_rows)
    if by_plane:
        above, below = near_rows[len(near) :]
        hops = [jnp.where(mp > chip, above, below)]
        if n_mp > 2:
            hops.append(along(hops[0], [(1, 2), (-1, -2)]))

    d_all = [d_query] + other_chips([d_query] * chips)
    spread = jnp.stack(around([d_kv] * n_mp))
    d_near = [d_all[k] for k in near]
    d_near, last = lax.optimization_barrier((d_near, hops[-1] if by_plane else x))
    for k, block in zip(near, d_near):
        d_all[k] = block
    for k, block in zip(near, near_rows):
        chip_rows[k] = block
    if by_plane:
        hops[-1] = last
        for hop in range(3, n_mp):
            hops.append(along(hops[-1], [(hop - 1, hop), (1 - hop, -hop)]))
        for hop, block in enumerate(hops, 1):
            far_rows = jnp.where(jnp.abs(mp - chip) == hop, block, far_rows)
        chip_rows.update(zip(rest, jnp.split(far_rows, len(rest))))
    else:
        chip_rows.update({k: flip(chip_rows[k], 2 * k) for k in rest})
    half = chip_width // 2
    early = [0] + near
    late = [k for k in range(chips) if k not in early]

    def product(some, which):
        mine = jnp.concatenate([chip_rows[k] for k in some])
        mine = lax.dynamic_slice_in_dim(mine, which * half, half, 1)
        theirs = jnp.concatenate([d_all[k] for k in some])
        return jnp.einsum("td,tc->dc", mine, theirs, preferred_element_type=F32)

    other = flip((product(early, 1 - core) + product(late, 1 - core)).astype(BF16), 1)
    grad_query = product(late, core) + (product(early, core) + other.astype(F32))

    if n_mp > KV_HEADS:
        spread = pick(spread, (mp - jnp.arange(n_mp)) % n_mp)
        spread = spread.reshape(KV_HEADS, n_mp // KV_HEADS, tokens, 2 * dim)
        spread = jnp.sum(spread.astype(F32), axis=1).astype(BF16)
        spread_at = lambda index: index
    else:
        spread_at = lambda index: (mp - index) % n_mp
    chip_cols = 2 * key_cols // chips
    if chip_cols != 2 * dim:
        spread = spread.reshape(KV_HEADS, tokens, chips // KV_HEADS, chip_cols)
        spread = spread.transpose(0, 2, 1, 3).reshape(chips, tokens, chip_cols)
    kv_all = [lax.dynamic_index_in_dim(spread, spread_at(chip ^ k), 0, False) for k in range(chips)]
    kv_all = jnp.stack([kv_all[0]] + other_chips(kv_all)).reshape(chips * tokens, chip_cols)
    partial = jnp.einsum("td,tc->dc", plane_rows, kv_all, preferred_element_type=F32)
    mine, theirs = partial[:, : chip_cols // 2], partial[:, chip_cols // 2 :]
    mine, theirs = jnp.where(core == 0, mine, theirs), jnp.where(core == 0, theirs, mine)
    grad_kv = mine + flip(theirs.astype(BF16), 1).astype(F32)
    device_cols = chip_cols // 4

    return (
        attended.reshape(slots, length, query_cols),
        grad_query,
        grad_kv[:, :device_cols],
        grad_kv[:, device_cols:],
    )


def solution(mesh):
    return jax.shard_map(
        functools.partial(local, mesh.shape["dp"], mesh.shape["mp"]),
        mesh=mesh,
        in_specs=(
            P("dp", None, "mp"),
            P("dp", None),
            P("dp"),
            P("dp"),
            P("dp"),
            P("dp", None, "mp"),
            P(None, "mp"),
            P("mp", None),
            P("mp", None),
            P(),
            P(),
        ),
        out_specs=(P("dp", None, "mp"), P("dp", "mp"), P("mp", "dp"), P("mp", "dp")),
        check_vma=False,
    )
```
